32 devices in a mesh: dp: 8 (over y, x, core), fsdp: 4 (over z).
Axes of the slice: x: 2, y: 2, z: 4, core: 2. Of those that a mesh axis runs over, the one named last changes fastest.
Arguments:
- hidden: bfloat16 [12288, 5120], P(('dp', 'fsdp')), may hold values from -6 to 6
- norm_gain: bfloat16 [5120], replicated, may hold values from 0.25 to 1.75
- q_weight: bfloat16 [5120, 2560], P('dp', 'fsdp')
- kv_weight: bfloat16 [5120, 1024], P('dp', 'fsdp')
- q_bias: bfloat16 [2560], replicated, may hold values from -3 to 3
- kv_bias: bfloat16 [1024], replicated, may hold values from -3 to 3
- segments: int32 [12288], P(('dp', 'fsdp')), may hold values from -1 to 383, as said below
Outputs:
- attention_context: bfloat16 [12288, 2560], P(('dp', 'fsdp'))
The draws below stay inside these ranges and needn't reach their ends.
Inputs may be any that keep to these rules, and one draw needn't show every extreme that they name: `segments`: in each device's run of 384 rows the live rows are its first whole blocks of 128; their ids start at 0 and never fall, each rollout has 1 to 256 rows, and somewhere in the slice one rollout has exactly 256; the other rows are -1. The devices at dp indices i and i + 8 / 2 with the same fsdp index hold exactly 4 live blocks together, and some device holds 3. Some device has 384 rollouts of one row each.
All inputs are finite; a program needn't handle non-finite values.
Results may differ from the reference program's by a relative error of at most 0.0058.
Values may be sent and summed in bfloat16 or wider, within the bound.
A program may use at most 128 MiB of HBM per device.

```python
import jax
import jax.numpy as jnp
from jax import lax

D = 5120
HEADS = 20
KV_HEADS = 4
HEAD_DIM = 128
BLOCK = 128
SLOTS = 3
MOST = 256
TOTAL_ROWS = 12288
QCOLS = 2560
KVCOLS = 1024
N_DP = 8
N_FSDP = 4


def key_columns(key):
    return jax.random.normal(jax.random.fold_in(key, 7), (D, 2 * KV_HEADS * HEAD_DIM), jnp.float32) * D ** (-0.5)


def draw_kv_weight(key, part):
    return key_columns(key).astype(jnp.bfloat16)


def draw_q_weight(key, part):
    base = jax.random.normal(jax.random.fold_in(key, 11), (D, HEADS * HEAD_DIM), jnp.float32) * D ** (-0.5)
    return base.astype(jnp.bfloat16)


def draw_segments(key, part):
    half_slots = (SLOTS + 1) // 2
    row_count = SLOTS * BLOCK
    device_count = N_DP * N_FSDP
    lower_loads = jax.random.randint(jax.random.fold_in(key, 3), (N_DP // 2, N_FSDP), 1, SLOTS + 1)
    lower_loads = lower_loads.at[0, 0].set(SLOTS)
    lower_loads = lower_loads.at[0, 1].set(SLOTS)
    block_loads = jnp.concatenate([lower_loads, 2 * half_slots - lower_loads], axis=0).reshape(-1)
    row_ids = jnp.arange(row_count, dtype=jnp.int32)[None, :]
    device_ids = jnp.arange(device_count, dtype=jnp.int32)[:, None]
    die_rolls = jax.random.randint(jax.random.fold_in(key, 5), (device_count, row_count), 0, 96)
    random_starts = (die_rolls == 0) & jnp.logical_not((device_ids == 1) & (row_ids < MOST))
    starts = random_starts | (row_ids % MOST == 0) | (device_ids == 0)
    segment_ids = jnp.cumsum(starts.astype(jnp.int32), axis=1) - 1
    live_rows = row_ids < block_loads[:, None] * BLOCK
    return jnp.where(live_rows, segment_ids, -1).astype(jnp.int32).reshape(-1)


def level_of(stream_key, shape, shards, low, top_value):
    factor_of = 1.0
    for position, parts in shards:
        draws = jax.random.uniform(jax.random.fold_in(jax.random.fold_in(stream_key, 6), position), (parts,), jnp.float32, low / len(shards), top_value / len(shards))
        factor_of = factor_of * jnp.repeat(jnp.exp(draws), shape[position] // parts).reshape((-1,) + (1,) * (len(shape) - 1 - position))
    return factor_of


def noise(stream_key, dims, deviation, bound, split=(), kind=jnp.bfloat16):
    drawn = jax.random.normal(stream_key, dims, jnp.float32) * deviation
    if len(split) > 0:
        drawn = level_of(stream_key, dims, split, -0.22, 0.18) * drawn
    return jnp.clip(drawn, min=-bound, max=bound).astype(kind)


def setup_inputs(seed: int = 0) -> dict:
    splits = jax.random.split(jax.random.key(seed), 8)
    return {
        "hidden": noise(splits[0], (TOTAL_ROWS, D), 1.0, 6.0, ((0, 32),)),
        "norm_gain": jnp.clip(1.0 + 0.15 * jax.random.normal(splits[1], (D,), jnp.float32), 0.25, 1.75).astype(jnp.bfloat16),
        "q_weight": draw_q_weight(jax.random.fold_in(splits[7], 71), 0),
        "kv_weight": draw_kv_weight(jax.random.fold_in(splits[7], 71), 0),
        "q_bias": noise(splits[4], (QCOLS,), 0.5, 3.0),
        "kv_bias": noise(splits[5], (KVCOLS,), 0.5, 3.0),
        "segments": draw_segments(jax.random.fold_in(splits[7], 71), 0),
    }


def positions_of(segments):
    row_ids = jnp.arange(segments.shape[0], dtype=jnp.int32)
    before = jnp.concatenate([jnp.full((1,), -3, jnp.int32), segments[:-1]])
    starts = jnp.where(segments != before, row_ids, 0).astype(jnp.int32)
    return row_ids - lax.cummax(starts, axis=0)

def rotate(source, positions):
    half_dim = HEAD_DIM // 2
    frequency = jnp.exp(jnp.arange(half_dim, dtype=jnp.float32) * (-2.0 / HEAD_DIM) * jnp.log(jnp.float32(1000000.0)))
    angles = positions.astype(jnp.float32)[:, None] * frequency[None, :]
    cosine = jnp.cos(angles)[:, None, :]
    sine_part = jnp.sin(angles)[:, None, :]
    lower_half = source[..., :half_dim]
    second = source[..., half_dim:]
    return jnp.concatenate([lower_half * cosine - second * sine_part, second * cosine + lower_half * sine_part], axis=-1)

def normalize(hidden, norm_gain):
    as_float = hidden.astype(jnp.float32)
    mean_square = lax.optimization_barrier(jnp.mean(as_float * as_float, axis=-1, keepdims=True))
    return (as_float * lax.rsqrt(mean_square + 1e-06) * norm_gain.astype(jnp.float32)).astype(jnp.bfloat16)

def windows(source, fill_value):
    block_count = source.shape[0] // BLOCK
    shaped = source.reshape((block_count, BLOCK) + source.shape[1:])
    padded = jnp.concatenate([jnp.full((2,) + shaped.shape[1:], fill_value, source.dtype), shaped], axis=0)
    return jnp.concatenate([padded[0:block_count], padded[1:block_count + 1], padded[2:block_count + 2]], axis=1)

def attend(queries, key_rows, values, segments):
    row_count = queries.shape[0]
    block_count = row_count // BLOCK
    group_size = HEADS // KV_HEADS
    row_ids = jnp.arange(row_count, dtype=jnp.int32)
    key_win = windows(key_rows, 0).astype(jnp.float32)
    value_win = windows(values, 0).astype(jnp.float32)
    seg_win = windows(segments, -2)
    row_win = windows(row_ids, -1)
    q_blocks = queries.reshape(block_count, BLOCK, KV_HEADS, group_size, HEAD_DIM).astype(jnp.float32)
    scores = jnp.einsum('bqkgd,bskd->bkgqs', q_blocks, key_win, precision=lax.Precision.HIGHEST) * HEAD_DIM ** (-0.5)
    q_seg = segments.reshape(block_count, BLOCK)
    q_row = row_ids.reshape(block_count, BLOCK)
    allowed = (seg_win[:, None, :] == q_seg[:, :, None]) & (row_win[:, None, :] <= q_row[:, :, None]) & (q_seg[:, :, None] >= 0)
    scores = jnp.where(allowed[:, None, None], scores, -1e+30)
    row_max = lax.optimization_barrier(jnp.max(scores, axis=-1, keepdims=True))
    exponents = jnp.exp(scores - row_max)
    probabilities = (exponents / lax.optimization_barrier(jnp.sum(exponents, axis=-1, keepdims=True))).astype(jnp.bfloat16)
    context = jnp.einsum('bkgqs,bskd->bqkgd', probabilities.astype(jnp.float32), value_win, precision=lax.Precision.HIGHEST)
    context = jnp.where((q_seg >= 0)[:, :, None, None, None], context, 0.0)
    return context.reshape(row_count, HEADS * HEAD_DIM).astype(jnp.bfloat16)

def one_device(hidden, segments, norm_gain, q_weight, kv_weight, q_bias, kv_bias):
    row_count = hidden.shape[0]
    positions = positions_of(segments)
    normed = normalize(hidden, norm_gain)
    q_lin = jnp.dot(normed, q_weight, preferred_element_type=jnp.float32) + q_bias.astype(jnp.float32)
    kv_lin = jnp.dot(normed, kv_weight, preferred_element_type=jnp.float32) + kv_bias.astype(jnp.float32)
    split_at = KV_HEADS * HEAD_DIM
    queries = rotate(q_lin.reshape(row_count, HEADS, HEAD_DIM), positions).astype(jnp.bfloat16)
    key_rows = rotate(kv_lin[:, :split_at].reshape(row_count, KV_HEADS, HEAD_DIM), positions).astype(jnp.bfloat16)
    values = kv_lin[:, split_at:].reshape(row_count, KV_HEADS, HEAD_DIM).astype(jnp.bfloat16)
    return attend(queries, key_rows, values, segments)

def reference(hidden, norm_gain, q_weight, kv_weight, q_bias, kv_bias, segments):
    run_rows = SLOTS * BLOCK
    device_count = hidden.shape[0] // run_rows
    hidden_runs = hidden.reshape(device_count, run_rows, hidden.shape[1])
    segment_runs = segments.reshape(device_count, run_rows)

    def single(items):
        return one_device(items[0], items[1], norm_gain, q_weight, kv_weight, q_bias, kv_bias)
    output = lax.map(single, (hidden_runs, segment_runs))
    return output.reshape(device_count * run_rows, HEADS * HEAD_DIM)
```

```python
import functools

import jax
import jax.numpy as jnp
from jax import lax
from jax.experimental import pallas as pl
from jax.experimental.pallas import tpu as pltpu
from jax.sharding import PartitionSpec as P

HEADS = 20
KV_HEADS = 4
HEAD_DIM = 128
BLOCK = 128
LANES = 128
MESH = pl.DeviceIdType.MESH
TO_X, TO_Y, TO_UP, TO_DOWN, TO_SIB = range(5)
OWN, VIA_X, VIA_Y, DIAG = range(4)


def gather_project_kernel(
    ndp, nz, pieces, late,
    hidden_ref, gain_ref, qw_ref, kvw_ref, qb_ref, kvb_ref, seg_ref,
    q_out, k_out, v_out,
    wbuf, raw, normed, acc, cos_t, sin_t, local_sem, send_sem, recv_sem,
):
    rows, width = raw.shape
    depth, qcols = qw_ref.shape
    kvcols = kvw_ref.shape[1]
    cols = qcols + kvcols
    step = depth // pieces
    me = lax.axis_index("dp")
    z = lax.axis_index("fsdp")
    core = lax.rem(me, 2)
    x = lax.rem(me // 2, 2)
    y = me // 4
    sib = me + 1 - 2 * core
    xn = me + 2 - 4 * x
    yn = me + 4 - 8 * y
    dg = xn + yn - me
    source = [me, xn, yn, dg]

    own_q = pltpu.make_async_copy(qw_ref, wbuf.at[me, z, :, pl.ds(0, qcols)], local_sem.at[0])
    own_kv = pltpu.make_async_copy(kvw_ref, wbuf.at[me, z, :, pl.ds(qcols, kvcols)], local_sem.at[1])
    load = pltpu.make_async_copy(hidden_ref, raw, local_sem.at[2])
    own_q.start()
    own_kv.start()
    load.start()

    barrier = pltpu.get_barrier_semaphore()
    for other in (sib, xn, yn):
        pl.semaphore_signal(barrier, inc=1, device_id=(other, z), device_id_type=MESH)

    @pl.when(z > 0)
    def _():
        pl.semaphore_signal(barrier, inc=1, device_id=(me, z - 1), device_id_type=MESH)

    @pl.when(z < nz - 1)
    def _():
        pl.semaphore_signal(barrier, inc=1, device_id=(me, z + 1), device_id_type=MESH)

    pl.semaphore_wait(barrier, 3 + jnp.minimum(z, 1) + jnp.minimum(nz - 1 - z, 1))
    own_q.wait()
    own_kv.wait()

    def copy(way, src, plane, k):
        piece = wbuf.at[src, plane, pl.ds(pl.multiple_of(k * step, step), step), :]
        target = {
            TO_X: (xn, z), TO_Y: (yn, z), TO_SIB: (sib, z),
            TO_UP: (me, z + 1), TO_DOWN: (me, z - 1),
        }[way]
        return pltpu.make_async_remote_copy(
            src_ref=piece, dst_ref=piece,
            send_sem=send_sem.at[way, src // 2, plane, k],
            recv_sem=recv_sem.at[src, plane, k],
            device_id=target, device_id_type=MESH,
        )

    def ways(rel, hop, sign):
        always = lambda k: True
        first = lambda k: lax.rem(k, 2) == 0
        second = lambda k: lax.rem(k, 2) == 1
        is_late = lambda k: k < late
        not_late = lambda k: k >= late
        found = []
        if hop == 0:
            up = always if rel == OWN else is_late
            found += [(TO_UP, up, z < nz - 1), (TO_DOWN, up, z > 0)]
            if rel == OWN:
                found += [(TO_X, always, True), (TO_Y, always, True)]
            if rel == VIA_X:
                found += [(TO_Y, first, True)]
            if rel == VIA_Y:
                found += [(TO_X, second, True)]
        else:
            onward = (TO_UP, z < nz - 1) if sign > 0 else (TO_DOWN, z > 0)
            found += [(onward[0], always if rel == OWN else is_late, onward[1])]
            if rel == OWN:
                found += [(TO_X, not_late, True), (TO_Y, not_late, True)]
            if rel == VIA_X:
                found += [(TO_Y, lambda k: (k >= late) & first(k), True)]
            if rel == VIA_Y:
                found += [(TO_X, lambda k: (k >= late) & second(k), True)]
        return found + [(TO_SIB, always, True)]

    def place(hop, sign):
        plane = z - sign * hop
        return plane, (plane >= 0) & (plane < nz)

    def both(a, b):
        if a is True:
            return b
        return a if b is True else a & b

    def guarded(cond, do):
        if cond is True:
            do()
        else:
            pl.when(cond)(do)

    def arrive(rel, hop, sign, k):
        plane, _ = place(hop, sign)
        src = source[rel]
        if not (rel == OWN and hop == 0):
            copy(TO_SIB, src, plane, k).wait_recv()
        for way, cond, reach in ways(rel, hop, sign):
            guarded(both(cond(k), reach), lambda way=way: copy(way, src, plane, k).start())

    def each(slots):
        def body(k, carry):
            for rel, hop, sign in slots:
                guarded(True if hop == 0 else place(hop, sign)[1],
                        lambda rel=rel, hop=hop, sign=sign: arrive(rel, hop, sign, k))
            return carry
        lax.fori_loop(0, pieces, body, 0)

    def signs(hop):
        return (1,) if hop == 0 else (1, -1)

    def multiply(hop, lane):
        for sign in signs(hop):
            plane, ok = place(hop, sign)

            def body(j, carry):
                base = lax.rem(me // 2 + j, ndp // 2) * 2
                src = base + (core if lane == 0 else 1 - core)
                if lane == 1:
                    def take(k, c):
                        copy(TO_SIB, src, plane, k).wait_recv()
                        return c
                    lax.fori_loop(0, pieces, take, 0)
                acc[plane] += jnp.dot(
                    normed[src], wbuf[src, plane], preferred_element_type=jnp.float32
                )
                return carry

            def run():
                lax.fori_loop(0, ndp // 2, body, 0)
            guarded(True if hop == 0 else ok, run)

    each([(OWN, 0, 1)])

    load.wait()
    group = 16

    def norm_rows(i, carry):
        at = pl.ds(pl.multiple_of(i * group, group), group)
        value = raw[at, :].astype(jnp.float32)
        mean = jnp.sum(value * value, axis=-1, keepdims=True) * (1.0 / width)
        scaled = value * lax.rsqrt(mean + 1e-06) * gain_ref[...].astype(jnp.float32)
        scaled = scaled.astype(jnp.bfloat16)
        for d in range(ndp):
            normed[d, at, :] = scaled[:, d * depth:(d + 1) * depth]
        return carry

    lax.fori_loop(0, rows // group, norm_rows, 0)
    for f in range(nz):
        acc[f, :, 0:qcols] = jnp.broadcast_to(
            qb_ref[:, f * qcols:(f + 1) * qcols].astype(jnp.float32), (rows, qcols))
        acc[f, :, qcols:cols] = jnp.broadcast_to(
            kvb_ref[:, f * kvcols:(f + 1) * kvcols].astype(jnp.float32), (rows, kvcols))
    each([(VIA_X, 0, 1), (VIA_Y, 0, 1)])

    seg_row = seg_ref[...].astype(jnp.float32)
    for b in range(rows // BLOCK):
        at = slice(b * BLOCK, (b + 1) * BLOCK)
        mine = jnp.transpose(jnp.broadcast_to(seg_row[:, at], (BLOCK, BLOCK)))[:, 0:1]
        ids = lax.broadcasted_iota(jnp.int32, (BLOCK, rows), 1).astype(jnp.float32)
        start = jnp.min(jnp.where(mine == seg_row, ids, float(rows)), axis=1, keepdims=True)
        here = (lax.broadcasted_iota(jnp.int32, (BLOCK, 1), 0) + b * BLOCK).astype(jnp.float32)
        position = here - start
        lane = lax.broadcasted_iota(jnp.int32, (BLOCK, HEAD_DIM), 1)
        half = HEAD_DIM // 2
        entry = jnp.where(lane < half, lane, lane - half).astype(jnp.float32)
        frequency = jnp.exp(entry * (-2.0 / HEAD_DIM) * jnp.log(jnp.float32(1000000.0)))
        angle = position * frequency
        cos_t[at, :] = jnp.cos(angle)
        sin_t[at, :] = jnp.where(lane < half, -1.0, 1.0) * jnp.sin(angle)

    for hop in range(nz):
        after = hop + 1
        if after < nz:
            each([(OWN, after, s) for s in signs(after)])
        if hop > 0:
            multiply(hop - 1, 1)
        each([(DIAG, hop, s) for s in signs(hop)])
        if after < nz:
            each([(r, after, s) for s in signs(after) for r in (VIA_X, VIA_Y)])
        multiply(hop, 0)
    multiply(nz - 1, 1)

    q_heads, kv_heads = qcols // HEAD_DIM, kvcols // HEAD_DIM

    def rotated(value, at):
        return (value * cos_t[at, :] + pltpu.roll(value, HEAD_DIM // 2, 1) * sin_t[at, :]).astype(jnp.bfloat16)

    def finish(b, carry):
        at = pl.ds(pl.multiple_of(b * BLOCK, BLOCK), BLOCK)
        for f in range(nz):
            for h in range(q_heads):
                g = f * q_heads + h
                q_out[at, g * HEAD_DIM:(g + 1) * HEAD_DIM] = rotated(
                    acc[f, at, h * HEAD_DIM:(h + 1) * HEAD_DIM], at)
            for h in range(kv_heads):
                g = f * kv_heads + h
                value = acc[f, at, qcols + h * HEAD_DIM:qcols + (h + 1) * HEAD_DIM]
                if g < nz * kv_heads // 2:
                    k_out[at, g * HEAD_DIM:(g + 1) * HEAD_DIM] = rotated(value, at)
                else:
                    g -= nz * kv_heads // 2
                    v_out[at, g * HEAD_DIM:(g + 1) * HEAD_DIM] = value.astype(jnp.bfloat16)
        return carry

    lax.fori_loop(0, rows // BLOCK, finish, 0)

    def drain(slots):
        def body(k, carry):
            for rel, hop, sign in slots:
                plane, ok = place(hop, sign)

                def wait_all(rel=rel, hop=hop, sign=sign, plane=plane):
                    for way, cond, reach in ways(rel, hop, sign):
                        guarded(both(cond(k), reach),
                                lambda way=way: copy(way, source[rel], plane, k).wait_send())
                guarded(True if hop == 0 else ok, wait_all)
            return carry
        lax.fori_loop(0, pieces, body, 0)

    for hop in range(nz):
        for s in signs(hop):
            drain([(r, hop, s) for r in (OWN, VIA_X, VIA_Y, DIAG)])


def gather_project(ndp, nz, hidden, norm_gain, q_weight, kv_weight, q_bias, kv_bias, seg):
    rows, width = hidden.shape
    depth, qcols = q_weight.shape
    kvcols = kv_weight.shape[1]
    pieces, late = 5, 1
    vmem = pl.BlockSpec(memory_space=pltpu.VMEM)
    hbm = pl.BlockSpec(memory_space=pl.ANY)
    bf16, f32 = jnp.bfloat16, jnp.float32
    return pl.pallas_call(
        functools.partial(gather_project_kernel, ndp, nz, pieces, late),
        out_shape=[
            jax.ShapeDtypeStruct((rows, qcols * nz), bf16),
            jax.ShapeDtypeStruct((rows, kvcols * nz // 2), bf16),
            jax.ShapeDtypeStruct((rows, kvcols * nz // 2), bf16),
        ],
        in_specs=[hbm, vmem, hbm, hbm, vmem, vmem, vmem],
        out_specs=[vmem] * 3,
        scratch_shapes=[
            pltpu.VMEM((ndp, nz, depth, qcols + kvcols), bf16),
            pltpu.VMEM((rows, width), bf16),
            pltpu.VMEM((ndp, rows, depth), bf16),
            pltpu.VMEM((nz, rows, qcols + kvcols), f32),
            pltpu.VMEM((rows, HEAD_DIM), f32),
            pltpu.VMEM((rows, HEAD_DIM), f32),
            pltpu.SemaphoreType.DMA((3,)),
            pltpu.SemaphoreType.DMA((5, ndp // 2, nz, pieces)),
            pltpu.SemaphoreType.DMA((ndp, nz, pieces)),
        ],
        compiler_params=pltpu.CompilerParams(
            collective_id=0, has_side_effects=True, vmem_limit_bytes=60 * 2**20),
        cost_estimate=pl.CostEstimate(
            flops=2 * rows * width * nz * (qcols + kvcols),
            bytes_accessed=2 * rows * width, transcendentals=0),
        name="gather_project",
    )(hidden, norm_gain.reshape(1, -1), q_weight, kv_weight,
      q_bias.reshape(1, -1), kv_bias.reshape(1, -1), seg)


def attend_kernel(q_ref, k_ref, v_ref, seg_ref, out_ref):
    rows = q_ref.shape[0]
    group = HEADS // KV_HEADS
    seg_row = seg_ref[...].astype(jnp.float32)
    for b in range(rows // BLOCK):
        at = slice(b * BLOCK, (b + 1) * BLOCK)
        seen = (b + 1) * BLOCK
        mine = jnp.transpose(jnp.broadcast_to(seg_row[:, at], (BLOCK, BLOCK)))[:, 0:1]
        r = lax.broadcasted_iota(jnp.int32, (BLOCK, seen), 0) + b * BLOCK
        s = lax.broadcasted_iota(jnp.int32, (BLOCK, seen), 1)
        allowed = (mine == seg_row[:, 0:seen]) & (s <= r) & (mine >= 0)
        live = mine >= 0

        def head_group(g, carry):
            kv_at = pl.ds(pl.multiple_of(g * HEAD_DIM, HEAD_DIM), HEAD_DIM)
            keys = k_ref[0:seen, kv_at]
            values = v_ref[0:seen, kv_at]
            for h in range(group):
                q_at = pl.ds(pl.multiple_of((g * group + h) * HEAD_DIM, HEAD_DIM), HEAD_DIM)
                scores = lax.dot_general(
                    q_ref[at, q_at], keys, (((1,), (1,)), ((), ())),
                    preferred_element_type=jnp.float32) * HEAD_DIM ** (-0.5)
                scores = jnp.where(allowed, scores, -1e30)
                e = jnp.exp(scores - jnp.max(scores, axis=-1, keepdims=True))
                p = (e * (1.0 / jnp.sum(e, axis=-1, keepdims=True))).astype(jnp.bfloat16)
                c = jnp.dot(p, values, preferred_element_type=jnp.float32)
                out_ref[at, q_at] = jnp.where(live, c, 0.0).astype(out_ref.dtype)
            return carry

        lax.fori_loop(0, KV_HEADS, head_group, 0)


def attend_rows(queries, key_rows, values, seg):
    vmem = pl.BlockSpec(memory_space=pltpu.VMEM)
    return pl.pallas_call(
        attend_kernel,
        out_shape=jax.ShapeDtypeStruct(queries.shape, jnp.bfloat16),
        in_specs=[vmem] * 4,
        out_specs=vmem,
        compiler_params=pltpu.CompilerParams(vmem_limit_bytes=32 * 2**20),
        name="attend_rows",
    )(queries, key_rows, values, seg)


def positions_of(segments):
    row_ids = jnp.arange(segments.shape[0], dtype=jnp.int32)
    before = jnp.concatenate([jnp.full((1,), -3, jnp.int32), segments[:-1]])
    starts = jnp.where(segments != before, row_ids, 0)
    return row_ids - lax.cummax(starts, axis=0)


def rotate(source, positions):
    half_dim = HEAD_DIM // 2
    frequency = jnp.exp(
        jnp.arange(half_dim, dtype=jnp.float32)
        * (-2.0 / HEAD_DIM)
        * jnp.log(jnp.float32(1000000.0))
    )
    angles = positions.astype(jnp.float32)[:, None] * frequency[None, :]
    cosine = jnp.cos(angles)[:, None, :]
    sine_part = jnp.sin(angles)[:, None, :]
    lower_half = source[..., :half_dim]
    second = source[..., half_dim:]
    return jnp.concatenate(
        [lower_half * cosine - second * sine_part, second * cosine + lower_half * sine_part],
        axis=-1,
    )


def normalize(hidden, norm_gain):
    as_float = hidden.astype(jnp.float32)
    mean_square = jnp.mean(as_float * as_float, axis=-1, keepdims=True)
    return (as_float * lax.rsqrt(mean_square + 1e-06) * norm_gain.astype(jnp.float32)).astype(
        jnp.bfloat16
    )


def windows(source, fill_value):
    block_count = source.shape[0] // BLOCK
    shaped = source.reshape((block_count, BLOCK) + source.shape[1:])
    padded = jnp.concatenate(
        [jnp.full((2,) + shaped.shape[1:], fill_value, source.dtype), shaped], axis=0
    )
    return jnp.concatenate(
        [padded[0:block_count], padded[1 : block_count + 1], padded[2 : block_count + 2]], axis=1
    )


def attend(queries, key_rows, values, segments):
    row_count = queries.shape[0]
    block_count = row_count // BLOCK
    group_size = HEADS // KV_HEADS
    row_ids = jnp.arange(row_count, dtype=jnp.int32)
    key_win = windows(key_rows, 0)
    value_win = windows(values, 0)
    seg_win = windows(segments, -2)
    row_win = windows(row_ids, -1)
    q_blocks = queries.reshape(block_count, BLOCK, KV_HEADS, group_size, HEAD_DIM)
    scores = jnp.einsum(
        "bqkgd,bskd->bkgqs", q_blocks, key_win, preferred_element_type=jnp.float32
    ) * HEAD_DIM ** (-0.5)
    q_seg = segments.reshape(block_count, BLOCK)
    q_row = row_ids.reshape(block_count, BLOCK)
    allowed = (
        (seg_win[:, None, :] == q_seg[:, :, None])
        & (row_win[:, None, :] <= q_row[:, :, None])
        & (q_seg[:, :, None] >= 0)
    )
    scores = jnp.where(allowed[:, None, None], scores, -1e30)
    row_max = jnp.max(scores, axis=-1, keepdims=True)
    exponents = jnp.exp(scores - row_max)
    probabilities = (exponents / jnp.sum(exponents, axis=-1, keepdims=True)).astype(jnp.bfloat16)
    context = jnp.einsum(
        "bkgqs,bskd->bqkgd", probabilities, value_win, preferred_element_type=jnp.float32
    )
    context = jnp.where((q_seg >= 0)[:, :, None, None, None], context, 0.0)
    return context.reshape(row_count, HEADS * HEAD_DIM).astype(jnp.bfloat16)


def project(row_input, positions, q_weight, kv_weight, q_bias, kv_bias):
    row_count = row_input.shape[0]
    q_rows_full, kv_rows_full = (
        lax.all_gather(q_weight, "fsdp", axis=1, tiled=True),
        lax.all_gather(kv_weight, "fsdp", axis=1, tiled=True),
    )

    def add_rows(piece_rows):
        return jnp.dot(row_input, piece_rows, preferred_element_type=jnp.float32)

    q_lin = add_rows(lax.all_gather(q_rows_full, "dp", axis=0, tiled=True))
    kv_lin = add_rows(lax.all_gather(kv_rows_full, "dp", axis=0, tiled=True))
    q_lin = q_lin + q_bias.astype(jnp.float32)
    kv_lin = kv_lin + kv_bias.astype(jnp.float32)
    split_at = KV_HEADS * HEAD_DIM
    queries = rotate(q_lin.reshape(row_count, HEADS, HEAD_DIM), positions).astype(jnp.bfloat16)
    key_rows = rotate(
        kv_lin[:, :split_at].reshape(row_count, KV_HEADS, HEAD_DIM), positions
    ).astype(jnp.bfloat16)
    values = kv_lin[:, split_at:].reshape(row_count, KV_HEADS, HEAD_DIM).astype(jnp.bfloat16)
    return (queries, key_rows, values)


def local(ndp, nz, hidden, norm_gain, q_weight, kv_weight, q_bias, kv_bias, segments):
    planes_fit = ndp == 2 * 2 * 2
    heads_fit = q_weight.shape[1] % HEAD_DIM == 0 and kv_weight.shape[1] % HEAD_DIM == 0
    if planes_fit and heads_fit:
        seg = segments.reshape(1, -1)
        queries, key_rows, values = gather_project(
            ndp, nz, hidden, norm_gain, q_weight, kv_weight, q_bias, kv_bias, seg)
        return attend_rows(queries, key_rows, values, seg)
    normed = normalize(hidden, norm_gain)
    positions = positions_of(segments)
    queries, key_rows, values = project(normed, positions, q_weight, kv_weight, q_bias, kv_bias)
    return attend(queries, key_rows, values, segments)


def solution(mesh):
    in_specs = (
        P(("dp", "fsdp"), None),
        P(),
        P("dp", "fsdp"),
        P("dp", "fsdp"),
        P(),
        P(),
        P(("dp", "fsdp")),
    )
    out_specs = P(("dp", "fsdp"), None)
    return jax.shard_map(
        functools.partial(local, mesh.shape["dp"], mesh.shape["fsdp"]), mesh=mesh, in_specs=in_specs, out_specs=out_specs, check_vma=False)
```

```python
import functools

import jax
import jax.numpy as jnp
from jax import lax
from jax.experimental import pallas as pl
from jax.experimental.pallas import tpu as pltpu
from jax.sharding import PartitionSpec as P

HEADS = 20
KV_HEADS = 4
HEAD_DIM = 128
BLOCK = 128
LANES = 128
MESH = pl.DeviceIdType.MESH
TO_X, TO_Y, TO_UP, TO_DOWN, TO_SIB = range(5)
OWN, VIA_X, VIA_Y, DIAG = range(4)
PIECE, LATE = range(2)


def gather_project_kernel(
    ndp, nz, pieces, late,
    hidden_ref, qw_ref, kvw_ref, small_ref,
    out_ref,
    wbuf, raw, normed, acc, cos_t, sin_t, mask_t, k_buf, v_buf, local_sem, send_sem, recv_sem,
):
    rows, width = raw.shape
    depth, qcols = qw_ref.shape
    kvcols = kvw_ref.shape[1]
    cols = qcols + kvcols
    qb_at = width
    kvb_at = qb_at + nz * qcols
    seg_at = kvb_at + nz * kvcols
    step = depth // pieces
    me = lax.axis_index("dp")
    z = lax.axis_index("fsdp")
    core = lax.rem(me, 2)
    x = lax.rem(me // 2, 2)
    y = me // 4
    sib = me + 1 - 2 * core
    xn = me + 2 - 4 * x
    yn = me + 4 - 8 * y
    dg = xn + yn - me
    source = [me, xn, yn, dg]

    own_q = pltpu.make_async_copy(qw_ref, wbuf.at[me, z, :, pl.ds(0, qcols)], local_sem.at[0])
    own_kv = pltpu.make_async_copy(kvw_ref, wbuf.at[me, z, :, pl.ds(qcols, kvcols)], local_sem.at[1])
    load = pltpu.make_async_copy(hidden_ref, raw, local_sem.at[2])
    own_q.start()
    own_kv.start()
    load.start()

    barrier = pltpu.get_barrier_semaphore()
    for other in (sib, xn, yn):
        pl.semaphore_signal(barrier, inc=1, device_id=(other, z), device_id_type=MESH)

    @pl.when(z > 0)
    def _():
        pl.semaphore_signal(barrier, inc=1, device_id=(me, z - 1), device_id_type=MESH)

    @pl.when(z < nz - 1)
    def _():
        pl.semaphore_signal(barrier, inc=1, device_id=(me, z + 1), device_id_type=MESH)

    pl.semaphore_wait(barrier, 3 + jnp.minimum(z, 1) + jnp.minimum(nz - 1 - z, 1))
    own_q.wait()
    own_kv.wait()

    def copy(way, src, plane, k):
        piece = wbuf.at[src, plane, pl.ds(pl.multiple_of(k * step, step), step), :]
        target = {
            TO_X: (xn, z), TO_Y: (yn, z), TO_SIB: (sib, z),
            TO_UP: (me, z + 1), TO_DOWN: (me, z - 1),
        }[way]
        return pltpu.make_async_remote_copy(
            src_ref=piece, dst_ref=piece,
            send_sem=send_sem.at[way, src // 2, plane, k],
            recv_sem=recv_sem.at[src, plane, k],
            device_id=target, device_id_type=MESH,
        )

    def ways(kind, rel, hop, sign):
        always = lambda k: True
        first = lambda k: lax.rem(k, 2) == 0
        second = lambda k: lax.rem(k, 2) == 1
        not_late = lambda k: k >= late
        up, down = (TO_UP, always, z < nz - 1), (TO_DOWN, always, z > 0)
        onward = up if sign > 0 else down
        sibling = (TO_SIB, always, True)
        if kind == LATE:
            return [up, down] if hop == 0 else [onward, sibling]
        if rel == OWN and hop == 0:
            return [up, down, (TO_X, always, True), (TO_Y, always, True), sibling]
        if rel == OWN:
            return [onward, (TO_X, not_late, True), (TO_Y, not_late, True), sibling]
        if rel == VIA_X:
            return [(TO_Y, first, True), sibling]
        if rel == VIA_Y:
            return [(TO_X, second, True), sibling]
        return [sibling]

    def place(hop, sign):
        plane = z - sign * hop
        return plane, (plane >= 0) & (plane < nz)

    def both(a, b):
        if a is True:
            return b
        return a if b is True else a & b

    def guarded(cond, do):
        if cond is True:
            do()
        else:
            pl.when(cond)(do)

    def span(kind, rel, hop):
        if kind == LATE:
            return 0, late
        return (0 if rel == OWN or hop == 0 else late), pieces

    def signs(hop):
        return (1,) if hop == 0 else (1, -1)

    def slots(kind, rels, hop):
        return [(kind, rel, hop, sign) for sign in signs(hop) for rel in rels]

    def arrive(kind, rel, hop, sign, k):
        plane, _ = place(hop, sign)
        src = source[rel]
        if hop > 0 or (rel != OWN and kind == PIECE):
            copy(TO_SIB, src, plane, k).wait_recv()
        for way, cond, reach in ways(kind, rel, hop, sign):
            guarded(both(cond(k), reach), lambda way=way: copy(way, src, plane, k).start())

    def each(todo, extra=None):
        low = min(span(*slot[:3])[0] for slot in todo)
        high = max(span(*slot[:3])[1] for slot in todo)

        def body(k, carry):
            for kind, rel, hop, sign in todo:
                begin, _ = span(kind, rel, hop)
                cond = True if hop == 0 else place(hop, sign)[1]
                if begin > low:
                    cond = both(k >= begin, cond)
                guarded(cond, lambda slot=(kind, rel, hop, sign): arrive(*slot, k))
            if extra is not None:
                count, work = extra
                per = -(-count // (high - low))

                def some(i, c):
                    work(i)
                    return c
                lax.fori_loop(jnp.minimum((k - low) * per, count),
                              jnp.minimum((k - low + 1) * per, count), some, 0)
            return carry
        lax.fori_loop(low, high, body, 0)

    def multiply_one(hop, sign, rel, lane):
        plane, ok = place(hop, sign)
        base = me + lax.rem(rel, 2) * (xn - me) + (rel // 2) * (yn - me)
        src = base + lane * (sib - me)

        def run():
            @pl.when(lane == 1)
            def _():
                def take(k, c):
                    copy(TO_SIB, src, plane, k).wait_recv()
                    return c
                lax.fori_loop(0, pieces, take, 0)
            acc[plane] += jnp.dot(
                normed[src], wbuf[src, plane], preferred_element_type=jnp.float32
            )
        guarded(True if hop == 0 else ok, run)

    def multiply(hop, lane, low=0, high=4):
        def body(i, carry):
            sign = 1 if hop == 0 else 1 - 2 * lax.rem(i, 2)
            rel = low + (i if hop == 0 else i // 2)
            multiply_one(hop, sign, rel, jnp.int32(lane))
            return carry
        lax.fori_loop(0, (high - low) * len(signs(hop)), body, 0)

    each(slots(PIECE, [OWN], 0))

    load.wait()
    group = 16

    def norm_rows(i, carry):
        at = pl.ds(pl.multiple_of(i * group, group), group)
        value = raw[at, :].astype(jnp.float32)
        mean = jnp.sum(value * value, axis=-1, keepdims=True) * (1.0 / width)
        scaled = value * lax.rsqrt(mean + 1e-06) * small_ref[:, 0:width]
        scaled = scaled.astype(jnp.bfloat16)
        for d in range(ndp):
            normed[d, at, :] = scaled[:, d * depth:(d + 1) * depth]
        return carry

    lax.fori_loop(0, rows // group, norm_rows, 0)
    for f in range(nz):
        acc[f, :, 0:qcols] = jnp.broadcast_to(
            small_ref[:, qb_at + f * qcols:qb_at + (f + 1) * qcols], (rows, qcols))
        acc[f, :, qcols:cols] = jnp.broadcast_to(
            small_ref[:, kvb_at + f * kvcols:kvb_at + (f + 1) * kvcols], (rows, kvcols))
    each(slots(PIECE, [VIA_X, VIA_Y], 0) + slots(PIECE, [OWN], 1))

    seg_row = small_ref[:, seg_at:seg_at + rows]
    for b in range(rows // BLOCK):
        at = slice(b * BLOCK, (b + 1) * BLOCK)
        mine = jnp.transpose(jnp.broadcast_to(seg_row[:, at], (BLOCK, BLOCK)))[:, 0:1]
        ids = lax.broadcasted_iota(jnp.int32, (BLOCK, rows), 1).astype(jnp.float32)
        start = jnp.min(jnp.where(mine == seg_row, ids, float(rows)), axis=1, keepdims=True)
        here = (lax.broadcasted_iota(jnp.int32, (BLOCK, 1), 0) + b * BLOCK).astype(jnp.float32)
        position = here - start
        lane = lax.broadcasted_iota(jnp.int32, (BLOCK, HEAD_DIM), 1)
        half = HEAD_DIM // 2
        entry = jnp.where(lane < half, lane, lane - half).astype(jnp.float32)
        frequency = jnp.exp(entry * (-2.0 / HEAD_DIM) * jnp.log(jnp.float32(1000000.0)))
        angle = position * frequency
        cos_t[at, :] = jnp.cos(angle)
        sin_t[at, :] = jnp.where(lane < half, -1.0, 1.0) * jnp.sin(angle)
        allowed = (mine == seg_row) & (ids <= here) & (mine >= 0.0)
        mask_t[at, 0:rows] = jnp.where(allowed, 1.0, 0.0)
        mask_t[at, rows:] = jnp.broadcast_to(jnp.where(mine >= 0.0, 1.0, 0.0), (BLOCK, LANES))

    group = HEADS // KV_HEADS
    key_planes = nz // 2
    per_plane = kvcols // HEAD_DIM

    def rotated(value, at):
        return (value * cos_t[at, :] + pltpu.roll(value, HEAD_DIM // 2, 1) * sin_t[at, :]).astype(jnp.bfloat16)

    def prepare(g):
        at = slice(0, rows)
        lanes = pl.ds(pl.multiple_of(qcols + lax.rem(g, per_plane) * HEAD_DIM, HEAD_DIM), HEAD_DIM)
        k_buf[g] = rotated(acc[g // per_plane, :, lanes], at)
        v_buf[g] = acc[key_planes + g // per_plane, :, lanes].astype(jnp.bfloat16)

    scale = HEAD_DIM ** (-0.5) * 1.4426950408889634

    def attend_head(g, h):
        lanes = pl.ds(pl.multiple_of(h * HEAD_DIM, HEAD_DIM), HEAD_DIM)
        out_lanes = pl.ds(pl.multiple_of((g * group + h) * HEAD_DIM, HEAD_DIM), HEAD_DIM)
        for b in range(rows // BLOCK):
            at = slice(b * BLOCK, (b + 1) * BLOCK)
            seen = (b + 1) * BLOCK
            query = rotated(acc[g, at, lanes], at)
            scores = lax.dot_general(
                query, k_buf[g, 0:seen, :], (((1,), (1,)), ((), ())),
                preferred_element_type=jnp.float32)
            scores = jnp.where(mask_t[at, 0:seen] > 0.5, scores * scale, -1e30)
            top = jnp.max(scores, axis=-1, keepdims=True)
            e = jnp.exp2(scores - top)
            share = mask_t[at, rows:rows + 1] / jnp.sum(e, axis=-1, keepdims=True)
            p = (e * share).astype(jnp.bfloat16)
            c = jnp.dot(p, v_buf[g, 0:seen, :], preferred_element_type=jnp.float32)
            out_ref[at, out_lanes] = c.astype(out_ref.dtype)

    def heads_of(first):
        def work(i):
            attend_head(first + i // group, lax.rem(i, group))
        return KV_HEADS // 2 * group, work

    near_first = (z // (nz // 2)) * (KV_HEADS // 2)
    far_first = KV_HEADS // 2 - near_first
    last = nz - 1

    each(slots(PIECE, [OWN], 2) + slots(PIECE, [DIAG], 0))
    multiply(0, 0)
    each(slots(PIECE, [VIA_X, VIA_Y], 1))
    each(slots(LATE, [VIA_X, VIA_Y, DIAG], 0))
    multiply(0, 1)
    each(slots(PIECE, [OWN], 3))
    each(slots(PIECE, [DIAG], 1))
    each(slots(LATE, [VIA_X, VIA_Y, DIAG], 1))
    multiply(1, 0)
    each(slots(PIECE, [VIA_X, VIA_Y], 2))
    multiply(1, 1)
    each(slots(LATE, [VIA_X, VIA_Y, DIAG], 2))
    each(slots(PIECE, [DIAG], 2))
    multiply(2, 0)
    multiply(2, 1)
    prepare(near_first)
    prepare(near_first + 1)
    each(slots(PIECE, [VIA_X, VIA_Y], last), heads_of(near_first))
    each(slots(LATE, [VIA_X, VIA_Y, DIAG], last))

    last_sign = 1 - 2 * jnp.int32(z < nz // 2)

    def far_shard(i):
        multiply_one(last, last_sign, lax.rem(i, 3), i // 3)

    each(slots(PIECE, [DIAG], last), (6, far_shard))
    multiply_one(last, last_sign, jnp.int32(DIAG), jnp.int32(0))
    multiply_one(last, last_sign, jnp.int32(DIAG), jnp.int32(1))
    prepare(far_first)
    prepare(far_first + 1)
    count, work = heads_of(far_first)

    def rest(i, carry):
        work(i)
        return carry
    lax.fori_loop(0, count, rest, 0)

    def drain(todo):
        def body(k, carry):
            for kind, rel, hop, sign in todo:
                plane, ok = place(hop, sign)
                begin, end = span(kind, rel, hop)
                cond = True if hop == 0 else ok
                if begin > 0:
                    cond = both(k >= begin, cond)
                if end < pieces:
                    cond = both(k < end, cond)

                def wait_all(kind=kind, rel=rel, hop=hop, sign=sign, plane=plane):
                    for way, sent, reach in ways(kind, rel, hop, sign):
                        guarded(both(sent(k), reach),
                                lambda way=way: copy(way, source[rel], plane, k).wait_send())
                guarded(cond, wait_all)
            return carry
        lax.fori_loop(0, pieces, body, 0)

    for hop in range(nz):
        drain(slots(PIECE, [OWN, VIA_X, VIA_Y, DIAG], hop) + slots(LATE, [VIA_X, VIA_Y, DIAG], hop))


def gather_project(ndp, nz, hidden, norm_gain, q_weight, kv_weight, q_bias, kv_bias, segments):
    rows, width = hidden.shape
    depth, qcols = q_weight.shape
    kvcols = kv_weight.shape[1]
    pieces, late = 10, 2
    vmem = pl.BlockSpec(memory_space=pltpu.VMEM)
    hbm = pl.BlockSpec(memory_space=pl.ANY)
    bf16, f32 = jnp.bfloat16, jnp.float32
    small = jnp.concatenate(
        [part.astype(f32) for part in (norm_gain, q_bias, kv_bias, segments)]).reshape(1, -1)
    return pl.pallas_call(
        functools.partial(gather_project_kernel, ndp, nz, pieces, late),
        out_shape=jax.ShapeDtypeStruct((rows, qcols * nz), bf16),
        in_specs=[hbm, hbm, hbm, vmem],
        out_specs=vmem,
        scratch_shapes=[
            pltpu.VMEM((ndp, nz, depth, qcols + kvcols), bf16),
            pltpu.VMEM((rows, width), bf16),
            pltpu.VMEM((ndp, rows, depth), bf16),
            pltpu.VMEM((nz, rows, qcols + kvcols), f32),
            pltpu.VMEM((rows, HEAD_DIM), f32),
            pltpu.VMEM((rows, HEAD_DIM), f32),
            pltpu.VMEM((rows, rows + LANES), f32),
            pltpu.VMEM((KV_HEADS, rows, HEAD_DIM), bf16),
            pltpu.VMEM((KV_HEADS, rows, HEAD_DIM), bf16),
            pltpu.SemaphoreType.DMA((3,)),
            pltpu.SemaphoreType.DMA((5, ndp // 2, nz, pieces)),
            pltpu.SemaphoreType.DMA((ndp, nz, pieces)),
        ],
        compiler_params=pltpu.CompilerParams(
            collective_id=0, has_side_effects=True, vmem_limit_bytes=60 * 2**20),
        cost_estimate=pl.CostEstimate(
            flops=2 * rows * width * nz * (qcols + kvcols),
            bytes_accessed=2 * rows * width, transcendentals=0),
        name="gather_project_attend",
    )(hidden, q_weight, kv_weight, small)


def positions_of(segments):
    row_ids = jnp.arange(segments.shape[0], dtype=jnp.int32)
    before = jnp.concatenate([jnp.full((1,), -3, jnp.int32), segments[:-1]])
    starts = jnp.where(segments != before, row_ids, 0)
    return row_ids - lax.cummax(starts, axis=0)


def rotate(source, positions):
    half_dim = HEAD_DIM // 2
    frequency = jnp.exp(
        jnp.arange(half_dim, dtype=jnp.float32)
        * (-2.0 / HEAD_DIM)
        * jnp.log(jnp.float32(1000000.0))
    )
    angles = positions.astype(jnp.float32)[:, None] * frequency[None, :]
    cosine = jnp.cos(angles)[:, None, :]
    sine_part = jnp.sin(angles)[:, None, :]
    lower_half = source[..., :half_dim]
    second = source[..., half_dim:]
    return jnp.concatenate(
        [lower_half * cosine - second * sine_part, second * cosine + lower_half * sine_part],
        axis=-1,
    )


def normalize(hidden, norm_gain):
    as_float = hidden.astype(jnp.float32)
    mean_square = jnp.mean(as_float * as_float, axis=-1, keepdims=True)
    return (as_float * lax.rsqrt(mean_square + 1e-06) * norm_gain.astype(jnp.float32)).astype(
        jnp.bfloat16
    )


def windows(source, fill_value):
    block_count = source.shape[0] // BLOCK
    shaped = source.reshape((block_count, BLOCK) + source.shape[1:])
    padded = jnp.concatenate(
        [jnp.full((2,) + shaped.shape[1:], fill_value, source.dtype), shaped], axis=0
    )
    return jnp.concatenate(
        [padded[0:block_count], padded[1 : block_count + 1], padded[2 : block_count + 2]], axis=1
    )


def attend(queries, key_rows, values, segments):
    row_count = queries.shape[0]
    block_count = row_count // BLOCK
    group_size = HEADS // KV_HEADS
    row_ids = jnp.arange(row_count, dtype=jnp.int32)
    key_win = windows(key_rows, 0)
    value_win = windows(values, 0)
    seg_win = windows(segments, -2)
    row_win = windows(row_ids, -1)
    q_blocks = queries.reshape(block_count, BLOCK, KV_HEADS, group_size, HEAD_DIM)
    scores = jnp.einsum(
        "bqkgd,bskd->bkgqs", q_blocks, key_win, preferred_element_type=jnp.float32
    ) * HEAD_DIM ** (-0.5)
    q_seg = segments.reshape(block_count, BLOCK)
    q_row = row_ids.reshape(block_count, BLOCK)
    allowed = (
        (seg_win[:, None, :] == q_seg[:, :, None])
        & (row_win[:, None, :] <= q_row[:, :, None])
        & (q_seg[:, :, None] >= 0)
    )
    scores = jnp.where(allowed[:, None, None], scores, -1e30)
    row_max = jnp.max(scores, axis=-1, keepdims=True)
    exponents = jnp.exp(scores - row_max)
    probabilities = (exponents / jnp.sum(exponents, axis=-1, keepdims=True)).astype(jnp.bfloat16)
    context = jnp.einsum(
        "bkgqs,bskd->bqkgd", probabilities, value_win, preferred_element_type=jnp.float32
    )
    context = jnp.where((q_seg >= 0)[:, :, None, None, None], context, 0.0)
    return context.reshape(row_count, HEADS * HEAD_DIM).astype(jnp.bfloat16)


def project(row_input, positions, q_weight, kv_weight, q_bias, kv_bias):
    row_count = row_input.shape[0]
    q_rows_full, kv_rows_full = (
        lax.all_gather(q_weight, "fsdp", axis=1, tiled=True),
        lax.all_gather(kv_weight, "fsdp", axis=1, tiled=True),
    )

    def add_rows(piece_rows):
        return jnp.dot(row_input, piece_rows, preferred_element_type=jnp.float32)

    q_lin = add_rows(lax.all_gather(q_rows_full, "dp", axis=0, tiled=True))
    kv_lin = add_rows(lax.all_gather(kv_rows_full, "dp", axis=0, tiled=True))
    q_lin = q_lin + q_bias.astype(jnp.float32)
    kv_lin = kv_lin + kv_bias.astype(jnp.float32)
    split_at = KV_HEADS * HEAD_DIM
    queries = rotate(q_lin.reshape(row_count, HEADS, HEAD_DIM), positions).astype(jnp.bfloat16)
    key_rows = rotate(
        kv_lin[:, :split_at].reshape(row_count, KV_HEADS, HEAD_DIM), positions
    ).astype(jnp.bfloat16)
    values = kv_lin[:, split_at:].reshape(row_count, KV_HEADS, HEAD_DIM).astype(jnp.bfloat16)
    return (queries, key_rows, values)


def local(ndp, nz, hidden, norm_gain, q_weight, kv_weight, q_bias, kv_bias, segments):
    planes_fit = ndp == 2 * 2 * 2
    heads_fit = (
        nz == KV_HEADS
        and q_weight.shape[1] == HEADS // KV_HEADS * HEAD_DIM
        and kv_weight.shape[1] == 2 * HEAD_DIM
    )
    if planes_fit and heads_fit:
        return gather_project(
            ndp, nz, hidden, norm_gain, q_weight, kv_weight, q_bias, kv_bias, segments)
    normed = normalize(hidden, norm_gain)
    positions = positions_of(segments)
    queries, key_rows, values = project(normed, positions, q_weight, kv_weight, q_bias, kv_bias)
    return attend(queries, key_rows, values, segments)


def solution(mesh):
    in_specs = (
        P(("dp", "fsdp"), None),
        P(),
        P("dp", "fsdp"),
        P("dp", "fsdp"),
        P(),
        P(),
        P(("dp", "fsdp")),
    )
    out_specs = P(("dp", "fsdp"), None)
    return jax.shard_map(
        functools.partial(local, mesh.shape["dp"], mesh.shape["fsdp"]), mesh=mesh, in_specs=in_specs, out_specs=out_specs, check_vma=False)
```

```python
import functools

import jax
import jax.numpy as jnp
from jax import lax
from jax.experimental import pallas as pl
from jax.experimental.pallas import tpu as pltpu
from jax.sharding import PartitionSpec as P

HEADS = 20
KV_HEADS = 4
HEAD_DIM = 128
BLOCK = 128
LANES = 128
MESH = pl.DeviceIdType.MESH
TO_X, TO_Y, TO_UP, TO_DOWN = range(4)
OWN, VIA_X, VIA_Y, DIAG = range(4)
PIECE, LATE = range(2)


def gather_project_kernel(
    ndp, nz, pieces, late,
    hidden_ref, qw_ref, kvw_ref, small_ref,
    out_ref,
    wbuf, raw, normed, acc, cos_t, sin_t, mask_t, k_buf, v_buf, local_sem, send_sem, share_sem, recv_sem,
):
    rows, width = raw.shape
    depth, qcols = qw_ref.shape
    kvcols = kvw_ref.shape[1]
    cols = qcols + kvcols
    qb_at = width
    kvb_at = qb_at + nz * qcols
    seg_at = kvb_at + nz * kvcols
    step = depth // pieces
    me = lax.axis_index("dp")
    z = lax.axis_index("fsdp")
    core = lax.rem(me, 2)
    x = lax.rem(me // 2, 2)
    y = me // 4
    sib = me + 1 - 2 * core
    xn = me + 2 - 4 * x
    yn = me + 4 - 8 * y
    dg = xn + yn - me
    source = [me, xn, yn, dg]

    own_q = pltpu.make_async_copy(qw_ref, wbuf.at[me, z, :, pl.ds(0, qcols)], local_sem.at[0])
    own_kv = pltpu.make_async_copy(kvw_ref, wbuf.at[me, z, :, pl.ds(qcols, kvcols)], local_sem.at[1])
    load = pltpu.make_async_copy(hidden_ref, raw, local_sem.at[2])
    own_q.start()
    own_kv.start()
    load.start()

    barrier = pltpu.get_barrier_semaphore()
    for other in (sib, xn, yn):
        pl.semaphore_signal(barrier, inc=1, device_id=(other, z), device_id_type=MESH)

    @pl.when(z > 0)
    def _():
        pl.semaphore_signal(barrier, inc=1, device_id=(me, z - 1), device_id_type=MESH)

    @pl.when(z < nz - 1)
    def _():
        pl.semaphore_signal(barrier, inc=1, device_id=(me, z + 1), device_id_type=MESH)

    pl.semaphore_wait(barrier, 3 + jnp.minimum(z, 1) + jnp.minimum(nz - 1 - z, 1))
    own_q.wait()
    own_kv.wait()

    def copy(way, src, plane, k):
        piece = wbuf.at[src, plane, pl.ds(pl.multiple_of(k * step, step), step), :]
        target = {
            TO_X: (xn, z), TO_Y: (yn, z), TO_UP: (me, z + 1), TO_DOWN: (me, z - 1),
        }[way]
        return pltpu.make_async_remote_copy(
            src_ref=piece, dst_ref=piece,
            send_sem=send_sem.at[way, plane],
            recv_sem=recv_sem.at[src, plane, k],
            device_id=target, device_id_type=MESH,
        )

    def shared(src, plane):
        shard = wbuf.at[src, plane]
        return pltpu.make_async_remote_copy(
            src_ref=shard, dst_ref=shard,
            send_sem=share_sem, recv_sem=recv_sem.at[src, plane, 0],
            device_id=(sib, z), device_id_type=MESH,
        )

    def ways(kind, rel, hop, sign):
        always = lambda k: True
        first = lambda k: lax.rem(k, 2) == 0
        second = lambda k: lax.rem(k, 2) == 1
        not_late = lambda k: k >= late
        up, down = (TO_UP, always, z < nz - 1), (TO_DOWN, always, z > 0)
        onward = up if sign > 0 else down
        if kind == LATE:
            return [up, down] if hop == 0 else [onward]
        if rel == OWN and hop == 0:
            return [up, down, (TO_X, always, True), (TO_Y, always, True)]
        if rel == OWN:
            return [onward, (TO_X, not_late, True), (TO_Y, not_late, True)]
        if rel == VIA_X:
            return [(TO_Y, first, True)]
        if rel == VIA_Y:
            return [(TO_X, second, True)]
        return []

    def place(hop, sign):
        plane = z - sign * hop
        return plane, (plane >= 0) & (plane < nz)

    def both(a, b):
        if a is True:
            return b
        return a if b is True else a & b

    def guarded(cond, do):
        if cond is True:
            do()
        else:
            pl.when(cond)(do)

    def span(kind, rel, hop):
        if kind == LATE:
            return 0, late
        return (0 if rel == OWN or hop == 0 else late), pieces

    def signs(hop):
        return (1,) if hop == 0 else (1, -1)

    def slots(kind, rels, hop):
        return [(kind, rel, hop, sign) for sign in signs(hop) for rel in rels]

    def arrive(kind, rel, hop, sign, k):
        plane, _ = place(hop, sign)
        src = source[rel]
        if hop > 0 or (rel != OWN and kind == PIECE):
            copy(TO_X, src, plane, k).wait_recv()
        for way, cond, reach in ways(kind, rel, hop, sign):
            guarded(both(cond(k), reach), lambda way=way: copy(way, src, plane, k).start())

    def each(todo, extra=None):
        low = min(span(*slot[:3])[0] for slot in todo)
        high = max(span(*slot[:3])[1] for slot in todo)

        def body(k, carry):
            for kind, rel, hop, sign in todo:
                begin, _ = span(kind, rel, hop)
                cond = True if hop == 0 else place(hop, sign)[1]
                if begin > low:
                    cond = both(k >= begin, cond)
                guarded(cond, lambda slot=(kind, rel, hop, sign): arrive(*slot, k))
            if extra is not None:
                count, work = extra
                per = -(-count // (high - low))

                def some(i, c):
                    work(i)
                    return c
                lax.fori_loop(jnp.minimum((k - low) * per, count),
                              jnp.minimum((k - low + 1) * per, count), some, 0)
            return carry
        lax.fori_loop(low, high, body, 0)

    def share(rels, hop):
        for sign in signs(hop):
            plane, ok = place(hop, sign)

            def send(plane=plane):
                for rel in rels:
                    shared(source[rel], plane).start()
            guarded(True if hop == 0 else ok, send)

    def multiply_one(hop, sign, rel, lane):
        plane, ok = place(hop, sign)
        base = me + lax.rem(rel, 2) * (xn - me) + (rel // 2) * (yn - me)
        src = base + lane * (sib - me)

        def run():
            @pl.when(lane == 1)
            def _():
                shared(src, plane).wait_recv()
            acc[plane] += jnp.dot(
                normed[src], wbuf[src, plane], preferred_element_type=jnp.float32
            )
        guarded(True if hop == 0 else ok, run)

    def multiply(hop, lane, low=0, high=4):
        def body(i, carry):
            sign = 1 if hop == 0 else 1 - 2 * lax.rem(i, 2)
            rel = low + (i if hop == 0 else i // 2)
            multiply_one(hop, sign, rel, jnp.int32(lane))
            return carry
        lax.fori_loop(0, (high - low) * len(signs(hop)), body, 0)

    each(slots(PIECE, [OWN], 0))
    share([OWN], 0)

    load.wait()
    group = 16

    def norm_rows(i, carry):
        at = pl.ds(pl.multiple_of(i * group, group), group)
        value = raw[at, :].astype(jnp.float32)
        mean = jnp.sum(value * value, axis=-1, keepdims=True) * (1.0 / width)
        scaled = value * lax.rsqrt(mean + 1e-06) * small_ref[:, 0:width]
        scaled = scaled.astype(jnp.bfloat16)
        for d in range(ndp):
            normed[d, at, :] = scaled[:, d * depth:(d + 1) * depth]
        return carry

    lax.fori_loop(0, rows // group, norm_rows, 0)
    for f in range(nz):
        acc[f, :, 0:qcols] = jnp.broadcast_to(
            small_ref[:, qb_at + f * qcols:qb_at + (f + 1) * qcols], (rows, qcols))
        acc[f, :, qcols:cols] = jnp.broadcast_to(
            small_ref[:, kvb_at + f * kvcols:kvb_at + (f + 1) * kvcols], (rows, kvcols))
    each(slots(PIECE, [VIA_X, VIA_Y], 0) + slots(PIECE, [OWN], 1))
    share([VIA_X, VIA_Y], 0)
    share([OWN], 1)

    seg_row = small_ref[:, seg_at:seg_at + rows]
    for b in range(rows // BLOCK):
        at = slice(b * BLOCK, (b + 1) * BLOCK)
        mine = jnp.transpose(jnp.broadcast_to(seg_row[:, at], (BLOCK, BLOCK)))[:, 0:1]
        ids = lax.broadcasted_iota(jnp.int32, (BLOCK, rows), 1).astype(jnp.float32)
        start = jnp.min(jnp.where(mine == seg_row, ids, float(rows)), axis=1, keepdims=True)
        here = (lax.broadcasted_iota(jnp.int32, (BLOCK, 1), 0) + b * BLOCK).astype(jnp.float32)
        position = here - start
        lane = lax.broadcasted_iota(jnp.int32, (BLOCK, HEAD_DIM), 1)
        half = HEAD_DIM // 2
        entry = jnp.where(lane < half, lane, lane - half).astype(jnp.float32)
        frequency = jnp.exp(entry * (-2.0 / HEAD_DIM) * jnp.log(jnp.float32(1000000.0)))
        angle = position * frequency
        cos_t[at, :] = jnp.cos(angle)
        sin_t[at, :] = jnp.where(lane < half, -1.0, 1.0) * jnp.sin(angle)
        allowed = (mine == seg_row) & (ids <= here) & (mine >= 0.0)
        mask_t[at, 0:rows] = jnp.where(allowed, 1.0, 0.0)
        mask_t[at, rows:] = jnp.broadcast_to(jnp.where(mine >= 0.0, 1.0, 0.0), (BLOCK, LANES))

    group = HEADS // KV_HEADS
    key_planes = nz // 2
    per_plane = kvcols // HEAD_DIM

    def rotated(value, at):
        return (value * cos_t[at, :] + pltpu.roll(value, HEAD_DIM // 2, 1) * sin_t[at, :]).astype(jnp.bfloat16)

    def prepare(g):
        at = slice(0, rows)
        lanes = pl.ds(pl.multiple_of(qcols + lax.rem(g, per_plane) * HEAD_DIM, HEAD_DIM), HEAD_DIM)
        k_buf[g] = rotated(acc[g // per_plane, :, lanes], at)
        v_buf[g] = acc[key_planes + g // per_plane, :, lanes].astype(jnp.bfloat16)

    scale = HEAD_DIM ** (-0.5) * 1.4426950408889634

    def attend_head(g, h):
        lanes = pl.ds(pl.multiple_of(h * HEAD_DIM, HEAD_DIM), HEAD_DIM)
        out_lanes = pl.ds(pl.multiple_of((g * group + h) * HEAD_DIM, HEAD_DIM), HEAD_DIM)
        for b in range(rows // BLOCK):
            at = slice(b * BLOCK, (b + 1) * BLOCK)
            seen = (b + 1) * BLOCK
            query = rotated(acc[g, at, lanes], at)
            scores = lax.dot_general(
                query, k_buf[g, 0:seen, :], (((1,), (1,)), ((), ())),
                preferred_element_type=jnp.float32)
            scores = jnp.where(mask_t[at, 0:seen] > 0.5, scores * scale, -1e30)
            top = jnp.max(scores, axis=-1, keepdims=True)
            e = jnp.exp2(scores - top)
            share = mask_t[at, rows:rows + 1] / jnp.sum(e, axis=-1, keepdims=True)
            p = (e * share).astype(jnp.bfloat16)
            c = jnp.dot(p, v_buf[g, 0:seen, :], preferred_element_type=jnp.float32)
            out_ref[at, out_lanes] = c.astype(out_ref.dtype)

    def heads_of(first):
        def work(i):
            attend_head(first + i // group, lax.rem(i, group))
        return KV_HEADS // 2 * group, work

    near_first = (z // (nz // 2)) * (KV_HEADS // 2)
    far_first = KV_HEADS // 2 - near_first
    last = nz - 1

    each(slots(PIECE, [OWN], 2) + slots(PIECE, [DIAG], 0))
    share([DIAG], 0)
    share([OWN], 2)
    multiply(0, 0)
    each(slots(PIECE, [VIA_X, VIA_Y], 1))
    each(slots(LATE, [VIA_X, VIA_Y, DIAG], 0))
    multiply(0, 1)
    each(slots(PIECE, [OWN], 3))
    share([OWN], 3)
    each(slots(PIECE, [DIAG], 1))
    each(slots(LATE, [VIA_X, VIA_Y, DIAG], 1))
    share([VIA_X, VIA_Y, DIAG], 1)
    multiply(1, 0)
    each(slots(PIECE, [VIA_X, VIA_Y], 2))
    multiply(1, 1)
    each(slots(LATE, [VIA_X, VIA_Y, DIAG], 2))
    each(slots(PIECE, [DIAG], 2))
    share([VIA_X, VIA_Y, DIAG], 2)
    multiply(2, 0)
    multiply(2, 1)
    prepare(near_first)
    prepare(near_first + 1)
    each(slots(PIECE, [VIA_X, VIA_Y], last), heads_of(near_first))
    each(slots(LATE, [VIA_X, VIA_Y, DIAG], last))
    share([VIA_X, VIA_Y], last)

    last_sign = 1 - 2 * jnp.int32(z < nz // 2)

    def far_shard(i):
        multiply_one(last, last_sign, lax.rem(i, 3), i // 3)

    each(slots(PIECE, [DIAG], last), (6, far_shard))
    share([DIAG], last)
    multiply_one(last, last_sign, jnp.int32(DIAG), jnp.int32(0))
    multiply_one(last, last_sign, jnp.int32(DIAG), jnp.int32(1))
    prepare(far_first)
    prepare(far_first + 1)
    count, work = heads_of(far_first)

    def rest(i, carry):
        work(i)
        return carry
    lax.fori_loop(0, count, rest, 0)

    def sent(way, plane, count):
        some = wbuf.at[pl.ds(0, count), 0, pl.ds(0, step), :]
        pltpu.make_async_copy(some, some, send_sem.at[way, plane]).wait()

    def flat(plane, carry):
        @pl.when(plane == z)
        def _():
            sent(TO_X, plane, pieces + pieces // 2)
            sent(TO_Y, plane, pieces + (pieces + 1) // 2)

        @pl.when(plane != z)
        def _():
            odd = pieces // 2 - late // 2
            sent(TO_X, plane, pieces - late + odd)
            sent(TO_Y, plane, pieces - late + (pieces - late - odd))

        @pl.when((plane <= z) & (z < nz - 1))
        def _():
            sent(TO_UP, plane, pieces + 3 * late)

        @pl.when((plane >= z) & (z > 0))
        def _():
            sent(TO_DOWN, plane, pieces + 3 * late)
        return carry

    lax.fori_loop(0, nz, flat, 0)
    lane_shards = wbuf.at[pl.ds(0, ndp // 2)]
    pltpu.make_async_copy(lane_shards, lane_shards, share_sem).wait()


def gather_project(ndp, nz, hidden, norm_gain, q_weight, kv_weight, q_bias, kv_bias, segments):
    rows, width = hidden.shape
    depth, qcols = q_weight.shape
    kvcols = kv_weight.shape[1]
    pieces, late = 5, 1
    vmem = pl.BlockSpec(memory_space=pltpu.VMEM)
    hbm = pl.BlockSpec(memory_space=pl.ANY)
    bf16, f32 = jnp.bfloat16, jnp.float32
    small = jnp.concatenate(
        [part.astype(f32) for part in (norm_gain, q_bias, kv_bias, segments)]).reshape(1, -1)
    return pl.pallas_call(
        functools.partial(gather_project_kernel, ndp, nz, pieces, late),
        out_shape=jax.ShapeDtypeStruct((rows, qcols * nz), bf16),
        in_specs=[hbm, hbm, hbm, vmem],
        out_specs=vmem,
        scratch_shapes=[
            pltpu.VMEM((ndp, nz, depth, qcols + kvcols), bf16),
            pltpu.VMEM((rows, width), bf16),
            pltpu.VMEM((ndp, rows, depth), bf16),
            pltpu.VMEM((nz, rows, qcols + kvcols), f32),
            pltpu.VMEM((rows, HEAD_DIM), f32),
            pltpu.VMEM((rows, HEAD_DIM), f32),
            pltpu.VMEM((rows, rows + LANES), f32),
            pltpu.VMEM((KV_HEADS, rows, HEAD_DIM), bf16),
            pltpu.VMEM((KV_HEADS, rows, HEAD_DIM), bf16),
            pltpu.SemaphoreType.DMA((3,)),
            pltpu.SemaphoreType.DMA((4, nz)),
            pltpu.SemaphoreType.DMA(()),
            pltpu.SemaphoreType.DMA((ndp, nz, pieces)),
        ],
        compiler_params=pltpu.CompilerParams(
            collective_id=0, has_side_effects=True, vmem_limit_bytes=60 * 2**20),
        cost_estimate=pl.CostEstimate(
            flops=2 * rows * width * nz * (qcols + kvcols),
            bytes_accessed=2 * rows * width, transcendentals=0),
        name="gather_project_attend",
    )(hidden, q_weight, kv_weight, small)


def positions_of(segments):
    row_ids = jnp.arange(segments.shape[0], dtype=jnp.int32)
    before = jnp.concatenate([jnp.full((1,), -3, jnp.int32), segments[:-1]])
    starts = jnp.where(segments != before, row_ids, 0)
    return row_ids - lax.cummax(starts, axis=0)


def rotate(source, positions):
    half_dim = HEAD_DIM // 2
    frequency = jnp.exp(
        jnp.arange(half_dim, dtype=jnp.float32)
        * (-2.0 / HEAD_DIM)
        * jnp.log(jnp.float32(1000000.0))
    )
    angles = positions.astype(jnp.float32)[:, None] * frequency[None, :]
    cosine = jnp.cos(angles)[:, None, :]
    sine_part = jnp.sin(angles)[:, None, :]
    lower_half = source[..., :half_dim]
    second = source[..., half_dim:]
    return jnp.concatenate(
        [lower_half * cosine - second * sine_part, second * cosine + lower_half * sine_part],
        axis=-1,
    )


def normalize(hidden, norm_gain):
    as_float = hidden.astype(jnp.float32)
    mean_square = jnp.mean(as_float * as_float, axis=-1, keepdims=True)
    return (as_float * lax.rsqrt(mean_square + 1e-06) * norm_gain.astype(jnp.float32)).astype(
        jnp.bfloat16
    )


def windows(source, fill_value):
    block_count = source.shape[0] // BLOCK
    shaped = source.reshape((block_count, BLOCK) + source.shape[1:])
    padded = jnp.concatenate(
        [jnp.full((2,) + shaped.shape[1:], fill_value, source.dtype), shaped], axis=0
    )
    return jnp.concatenate(
        [padded[0:block_count], padded[1 : block_count + 1], padded[2 : block_count + 2]], axis=1
    )


def attend(queries, key_rows, values, segments):
    row_count = queries.shape[0]
    block_count = row_count // BLOCK
    group_size = HEADS // KV_HEADS
    row_ids = jnp.arange(row_count, dtype=jnp.int32)
    key_win = windows(key_rows, 0)
    value_win = windows(values, 0)
    seg_win = windows(segments, -2)
    row_win = windows(row_ids, -1)
    q_blocks = queries.reshape(block_count, BLOCK, KV_HEADS, group_size, HEAD_DIM)
    scores = jnp.einsum(
        "bqkgd,bskd->bkgqs", q_blocks, key_win, preferred_element_type=jnp.float32
    ) * HEAD_DIM ** (-0.5)
    q_seg = segments.reshape(block_count, BLOCK)
    q_row = row_ids.reshape(block_count, BLOCK)
    allowed = (
        (seg_win[:, None, :] == q_seg[:, :, None])
        & (row_win[:, None, :] <= q_row[:, :, None])
        & (q_seg[:, :, None] >= 0)
    )
    scores = jnp.where(allowed[:, None, None], scores, -1e30)
    row_max = jnp.max(scores, axis=-1, keepdims=True)
    exponents = jnp.exp(scores - row_max)
    probabilities = (exponents / jnp.sum(exponents, axis=-1, keepdims=True)).astype(jnp.bfloat16)
    context = jnp.einsum(
        "bkgqs,bskd->bqkgd", probabilities, value_win, preferred_element_type=jnp.float32
    )
    context = jnp.where((q_seg >= 0)[:, :, None, None, None], context, 0.0)
    return context.reshape(row_count, HEADS * HEAD_DIM).astype(jnp.bfloat16)


def project(row_input, positions, q_weight, kv_weight, q_bias, kv_bias):
    row_count = row_input.shape[0]
    q_rows_full, kv_rows_full = (
        lax.all_gather(q_weight, "fsdp", axis=1, tiled=True),
        lax.all_gather(kv_weight, "fsdp", axis=1, tiled=True),
    )

    def add_rows(piece_rows):
        return jnp.dot(row_input, piece_rows, preferred_element_type=jnp.float32)

    q_lin = add_rows(lax.all_gather(q_rows_full, "dp", axis=0, tiled=True))
    kv_lin = add_rows(lax.all_gather(kv_rows_full, "dp", axis=0, tiled=True))
    q_lin = q_lin + q_bias.astype(jnp.float32)
    kv_lin = kv_lin + kv_bias.astype(jnp.float32)
    split_at = KV_HEADS * HEAD_DIM
    queries = rotate(q_lin.reshape(row_count, HEADS, HEAD_DIM), positions).astype(jnp.bfloat16)
    key_rows = rotate(
        kv_lin[:, :split_at].reshape(row_count, KV_HEADS, HEAD_DIM), positions
    ).astype(jnp.bfloat16)
    values = kv_lin[:, split_at:].reshape(row_count, KV_HEADS, HEAD_DIM).astype(jnp.bfloat16)
    return (queries, key_rows, values)


def local(ndp, nz, hidden, norm_gain, q_weight, kv_weight, q_bias, kv_bias, segments):
    planes_fit = ndp == 2 * 2 * 2
    heads_fit = (
        nz == KV_HEADS
        and q_weight.shape[1] == HEADS // KV_HEADS * HEAD_DIM
        and kv_weight.shape[1] == 2 * HEAD_DIM
    )
    if planes_fit and heads_fit:
        return gather_project(
            ndp, nz, hidden, norm_gain, q_weight, kv_weight, q_bias, kv_bias, segments)
    normed = normalize(hidden, norm_gain)
    positions = positions_of(segments)
    queries, key_rows, values = project(normed, positions, q_weight, kv_weight, q_bias, kv_bias)
    return attend(queries, key_rows, values, segments)


def solution(mesh):
    in_specs = (
        P(("dp", "fsdp"), None),
        P(),
        P("dp", "fsdp"),
        P("dp", "fsdp"),
        P(),
        P(),
        P(("dp", "fsdp")),
    )
    out_specs = P(("dp", "fsdp"), None)
    return jax.shard_map(
        functools.partial(local, mesh.shape["dp"], mesh.shape["fsdp"]), mesh=mesh, in_specs=in_specs, out_specs=out_specs, check_vma=False)
```

```python
import functools

import jax
import jax.numpy as jnp
from jax import lax
from jax.experimental import pallas as pl
from jax.experimental.pallas import tpu as pltpu
from jax.sharding import PartitionSpec as P

HEADS = 20
KV_HEADS = 4
HEAD_DIM = 128
BLOCK = 128
LANES = 128
MESH = pl.DeviceIdType.MESH
TO_X, TO_Y, TO_UP, TO_DOWN = range(4)
OWN, VIA_X, VIA_Y, DIAG = range(4)
PIECE, LATE = range(2)


def gather_project_kernel(
    ndp, nz, pieces, late,
    hidden_ref, qw_ref, kvw_ref, small_ref,
    out_ref,
    wbuf, raw, normed, acc, cos_t, sin_t, mask_t, k_buf, v_buf, local_sem, send_sem, share_sem, recv_sem,
):
    rows, width = raw.shape
    depth, qcols = qw_ref.shape
    kvcols = kvw_ref.shape[1]
    cols = qcols + kvcols
    qb_at = width
    kvb_at = qb_at + nz * qcols
    seg_at = kvb_at + nz * kvcols
    step = depth // pieces
    me = lax.axis_index("dp")
    z = lax.axis_index("fsdp")
    core = lax.rem(me, 2)
    x = lax.rem(me // 2, 2)
    y = me // 4
    sib = me + 1 - 2 * core
    xn = me + 2 - 4 * x
    yn = me + 4 - 8 * y
    dg = xn + yn - me
    source = [me, xn, yn, dg]

    own_q = pltpu.make_async_copy(qw_ref, wbuf.at[me, z, :, pl.ds(0, qcols)], local_sem.at[0])
    own_kv = pltpu.make_async_copy(kvw_ref, wbuf.at[me, z, :, pl.ds(qcols, kvcols)], local_sem.at[1])
    load = pltpu.make_async_copy(hidden_ref, raw, local_sem.at[2])
    own_q.start()
    own_kv.start()
    load.start()

    barrier = pltpu.get_barrier_semaphore()
    for other in (sib, xn, yn):
        pl.semaphore_signal(barrier, inc=1, device_id=(other, z), device_id_type=MESH)

    @pl.when(z > 0)
    def _():
        pl.semaphore_signal(barrier, inc=1, device_id=(me, z - 1), device_id_type=MESH)

    @pl.when(z < nz - 1)
    def _():
        pl.semaphore_signal(barrier, inc=1, device_id=(me, z + 1), device_id_type=MESH)

    pl.semaphore_wait(barrier, 3 + jnp.minimum(z, 1) + jnp.minimum(nz - 1 - z, 1))
    own_q.wait()
    own_kv.wait()

    def copy(way, src, plane, k):
        piece = wbuf.at[src, plane, pl.ds(pl.multiple_of(k * step, step), step), :]
        target = {
            TO_X: (xn, z), TO_Y: (yn, z), TO_UP: (me, z + 1), TO_DOWN: (me, z - 1),
        }[way]
        return pltpu.make_async_remote_copy(
            src_ref=piece, dst_ref=piece,
            send_sem=send_sem.at[way, plane],
            recv_sem=recv_sem.at[src, plane, k],
            device_id=target, device_id_type=MESH,
        )

    def shared(src, plane):
        shard = wbuf.at[src, plane]
        return pltpu.make_async_remote_copy(
            src_ref=shard, dst_ref=shard,
            send_sem=share_sem, recv_sem=recv_sem.at[src, plane, 0],
            device_id=(sib, z), device_id_type=MESH,
        )

    def ways(kind, rel, hop, sign):
        always = lambda k: True
        first = lambda k: lax.rem(k, 2) == 0
        second = lambda k: lax.rem(k, 2) == 1
        not_late = lambda k: k >= late
        up, down = (TO_UP, always, z < nz - 1), (TO_DOWN, always, z > 0)
        onward = up if sign > 0 else down
        if kind == LATE:
            return [up, down] if hop == 0 else [onward]
        if rel == OWN and hop == 0:
            return [up, down, (TO_X, always, True), (TO_Y, always, True)]
        if rel == OWN:
            return [onward, (TO_X, not_late, True), (TO_Y, not_late, True)]
        if rel == VIA_X:
            return [(TO_Y, first, True)]
        if rel == VIA_Y:
            return [(TO_X, second, True)]
        return []

    def place(hop, sign):
        plane = z - sign * hop
        return plane, (plane >= 0) & (plane < nz)

    def both(a, b):
        if a is True:
            return b
        return a if b is True else a & b

    def guarded(cond, do):
        if cond is True:
            do()
        else:
            pl.when(cond)(do)

    def span(kind, rel, hop):
        if kind == LATE:
            return 0, late
        return (0 if rel == OWN or hop == 0 else late), pieces

    def signs(hop):
        return (1,) if hop == 0 else (1, -1)

    def slots(kind, rels, hop):
        return [(kind, rel, hop, sign) for sign in signs(hop) for rel in rels]

    def arrive(kind, rel, hop, sign, k):
        plane, _ = place(hop, sign)
        src = source[rel]
        if hop > 0 or (rel != OWN and kind == PIECE):
            copy(TO_X, src, plane, k).wait_recv()
        for way, cond, reach in ways(kind, rel, hop, sign):
            guarded(both(cond(k), reach), lambda way=way: copy(way, src, plane, k).start())

    def each(todo, *extra):
        low = min(span(*slot[:3])[0] for slot in todo)
        high = max(span(*slot[:3])[1] for slot in todo)

        def body(k, carry):
            for kind, rel, hop, sign in todo:
                begin, _ = span(kind, rel, hop)
                cond = True if hop == 0 else place(hop, sign)[1]
                if begin > low:
                    cond = both(k >= begin, cond)
                guarded(cond, lambda slot=(kind, rel, hop, sign): arrive(*slot, k))
            for count, work in extra:
                per = -(-count // (high - low))

                def some(i, c, work=work):
                    work(i)
                    return c
                lax.fori_loop(jnp.minimum((k - low) * per, count),
                              jnp.minimum((k - low + 1) * per, count), some, 0)
            return carry
        lax.fori_loop(low, high, body, 0)

    def share(rels, hop):
        for sign in signs(hop):
            plane, ok = place(hop, sign)

            def send(plane=plane):
                for rel in rels:
                    shared(source[rel], plane).start()
            guarded(True if hop == 0 else ok, send)

    def multiply_one(hop, sign, rel, lane):
        plane, ok = place(hop, sign)
        base = me + lax.rem(rel, 2) * (xn - me) + (rel // 2) * (yn - me)
        src = base + lane * (sib - me)

        def run():
            @pl.when(lane == 1)
            def _():
                shared(src, plane).wait_recv()
            acc[plane] += jnp.dot(
                normed[src], wbuf[src, plane], preferred_element_type=jnp.float32
            )
        guarded(True if hop == 0 else ok, run)

    def shards(hop, low, high):
        ways_in, rels = len(signs(hop)), high - low

        def work(i):
            j = i // ways_in
            multiply_one(hop, 1 - 2 * lax.rem(i, ways_in), low + lax.rem(j, rels), j // rels)
        return ways_in * rels * 2, work

    def run_all(count, work):
        def body(i, carry):
            work(i)
            return carry
        lax.fori_loop(0, count, body, 0)

    each(slots(PIECE, [OWN], 0))
    share([OWN], 0)

    load.wait()
    group = 16

    def norm_rows(i, carry):
        at = pl.ds(pl.multiple_of(i * group, group), group)
        value = raw[at, :].astype(jnp.float32)
        mean = jnp.sum(value * value, axis=-1, keepdims=True) * (1.0 / width)
        scaled = value * lax.rsqrt(mean + 1e-06) * small_ref[:, 0:width]
        scaled = scaled.astype(jnp.bfloat16)
        for d in range(ndp):
            normed[d, at, :] = scaled[:, d * depth:(d + 1) * depth]
        return carry

    lax.fori_loop(0, rows // group, norm_rows, 0)
    for f in range(nz):
        acc[f, :, 0:qcols] = jnp.broadcast_to(
            small_ref[:, qb_at + f * qcols:qb_at + (f + 1) * qcols], (rows, qcols))
        acc[f, :, qcols:cols] = jnp.broadcast_to(
            small_ref[:, kvb_at + f * kvcols:kvb_at + (f + 1) * kvcols], (rows, kvcols))
    each(slots(PIECE, [VIA_X, VIA_Y], 0) + slots(PIECE, [OWN], 1))
    share([VIA_X, VIA_Y], 0)
    share([OWN], 1)

    seg_row = small_ref[:, seg_at:seg_at + rows]
    for b in range(rows // BLOCK):
        at = slice(b * BLOCK, (b + 1) * BLOCK)
        mine = jnp.transpose(jnp.broadcast_to(seg_row[:, at], (BLOCK, BLOCK)))[:, 0:1]
        ids = lax.broadcasted_iota(jnp.int32, (BLOCK, rows), 1).astype(jnp.float32)
        start = jnp.min(jnp.where(mine == seg_row, ids, float(rows)), axis=1, keepdims=True)
        here = (lax.broadcasted_iota(jnp.int32, (BLOCK, 1), 0) + b * BLOCK).astype(jnp.float32)
        position = here - start
        lane = lax.broadcasted_iota(jnp.int32, (BLOCK, HEAD_DIM), 1)
        half = HEAD_DIM // 2
        entry = jnp.where(lane < half, lane, lane - half).astype(jnp.float32)
        frequency = jnp.exp(entry * (-2.0 / HEAD_DIM) * jnp.log(jnp.float32(1000000.0)))
        angle = position * frequency
        cos_t[at, :] = jnp.cos(angle)
        sin_t[at, :] = jnp.where(lane < half, -1.0, 1.0) * jnp.sin(angle)
        allowed = (mine == seg_row) & (ids <= here) & (mine >= 0.0)
        mask_t[at, 0:rows] = jnp.where(allowed, 1.0, 0.0)
        mask_t[at, rows:] = jnp.broadcast_to(jnp.where(mine >= 0.0, 1.0, 0.0), (BLOCK, LANES))

    group = HEADS // KV_HEADS
    key_planes = nz // 2
    per_plane = kvcols // HEAD_DIM

    def rotated(value, at):
        return (value * cos_t[at, :] + pltpu.roll(value, HEAD_DIM // 2, 1) * sin_t[at, :]).astype(jnp.bfloat16)

    def prepare(g):
        at = slice(0, rows)
        lanes = pl.ds(pl.multiple_of(qcols + lax.rem(g, per_plane) * HEAD_DIM, HEAD_DIM), HEAD_DIM)
        k_buf[g] = rotated(acc[g // per_plane, :, lanes], at)
        v_buf[g] = acc[key_planes + g // per_plane, :, lanes].astype(jnp.bfloat16)

    scale = HEAD_DIM ** (-0.5) * 1.4426950408889634

    def attend_group(g):
        prepare(g)
        blocks = range(rows // BLOCK)
        scores, shares = [], []
        for b in blocks:
            at = slice(b * BLOCK, (b + 1) * BLOCK)
            seen = (b + 1) * BLOCK
            query = jnp.concatenate([
                rotated(acc[g, at, h * HEAD_DIM:(h + 1) * HEAD_DIM], at) for h in range(group)], axis=0)
            score = lax.dot_general(
                query, k_buf[g, 0:seen, :], (((1,), (1,)), ((), ())),
                preferred_element_type=jnp.float32).reshape(group, BLOCK, seen)
            scores.append(jnp.where(mask_t[at, 0:seen][None] > 0.5, score * scale, -1e30))
        tops = [jnp.max(score, axis=-1, keepdims=True) for score in scores]
        scores = [jnp.exp2(score - top) for score, top in zip(scores, tops)]
        sums = [jnp.sum(score, axis=-1, keepdims=True) for score in scores]
        for b in blocks:
            at = slice(b * BLOCK, (b + 1) * BLOCK)
            seen = (b + 1) * BLOCK
            share_of = mask_t[at, rows:rows + 1][None] / sums[b]
            p = (scores[b] * share_of).astype(jnp.bfloat16).reshape(group * BLOCK, seen)
            c = jnp.dot(p, v_buf[g, 0:seen, :], preferred_element_type=jnp.float32)
            for h in range(group):
                lanes = pl.ds(pl.multiple_of((g * group + h) * HEAD_DIM, HEAD_DIM), HEAD_DIM)
                out_ref[at, lanes] = c[h * BLOCK:(h + 1) * BLOCK].astype(out_ref.dtype)

    half_heads = KV_HEADS // 2
    near_first = (z // (nz // 2)) * half_heads
    far_first = half_heads - near_first

    each(slots(PIECE, [OWN], 2) + slots(PIECE, [DIAG], 0), shards(0, OWN, DIAG))
    share([DIAG], 0)
    share([OWN], 2)
    each(slots(PIECE, [VIA_X, VIA_Y], 1), shards(0, DIAG, DIAG + 1), shards(1, OWN, VIA_X))
    each(slots(LATE, [VIA_X, VIA_Y, DIAG], 0))
    each(slots(PIECE, [OWN], 3), shards(2, OWN, VIA_X))
    share([OWN], 3)
    each(slots(PIECE, [VIA_X, VIA_Y], 2), shards(3, OWN, VIA_X))
    each(slots(LATE, [VIA_X, VIA_Y, DIAG], 1))
    each(slots(PIECE, [DIAG], 1))
    share([VIA_X, VIA_Y, DIAG], 1)
    each(slots(LATE, [VIA_X, VIA_Y, DIAG], 2))
    each(slots(PIECE, [VIA_X, VIA_Y], 3), shards(1, VIA_X, DIAG + 1))
    each(slots(PIECE, [DIAG], 2))
    share([VIA_X, VIA_Y, DIAG], 2)
    each(slots(LATE, [VIA_X, VIA_Y, DIAG], 3))
    share([VIA_X, VIA_Y], 3)
    run_all(*shards(2, VIA_X, DIAG + 1))
    run_all(half_heads, lambda i: attend_group(near_first + i))
    each(slots(PIECE, [DIAG], 3), shards(3, VIA_X, DIAG))
    share([DIAG], 3)
    run_all(*shards(3, DIAG, DIAG + 1))
    run_all(half_heads, lambda i: attend_group(far_first + i))

    def sent(way, plane, count):
        some = wbuf.at[pl.ds(0, count), 0, pl.ds(0, step), :]
        pltpu.make_async_copy(some, some, send_sem.at[way, plane]).wait()

    def flat(plane, carry):
        @pl.when(plane == z)
        def _():
            sent(TO_X, plane, pieces + pieces // 2)
            sent(TO_Y, plane, pieces + (pieces + 1) // 2)

        @pl.when(plane != z)
        def _():
            odd = pieces // 2 - late // 2
            sent(TO_X, plane, pieces - late + odd)
            sent(TO_Y, plane, pieces - late + (pieces - late - odd))

        @pl.when((plane <= z) & (z < nz - 1))
        def _():
            sent(TO_UP, plane, pieces + 3 * late)

        @pl.when((plane >= z) & (z > 0))
        def _():
            sent(TO_DOWN, plane, pieces + 3 * late)
        return carry

    lax.fori_loop(0, nz, flat, 0)
    lane_shards = wbuf.at[pl.ds(0, ndp // 2)]
    pltpu.make_async_copy(lane_shards, lane_shards, share_sem).wait()


def gather_project(ndp, nz, hidden, norm_gain, q_weight, kv_weight, q_bias, kv_bias, segments):
    rows, width = hidden.shape
    depth, qcols = q_weight.shape
    kvcols = kv_weight.shape[1]
    pieces, late = 5, 1
    vmem = pl.BlockSpec(memory_space=pltpu.VMEM)
    hbm = pl.BlockSpec(memory_space=pl.ANY)
    bf16, f32 = jnp.bfloat16, jnp.float32
    small = jnp.concatenate(
        [part.astype(f32) for part in (norm_gain, q_bias, kv_bias, segments)]).reshape(1, -1)
    return pl.pallas_call(
        functools.partial(gather_project_kernel, ndp, nz, pieces, late),
        out_shape=jax.ShapeDtypeStruct((rows, qcols * nz), bf16),
        in_specs=[hbm, hbm, hbm, vmem],
        out_specs=vmem,
        scratch_shapes=[
            pltpu.VMEM((ndp, nz, depth, qcols + kvcols), bf16),
            pltpu.VMEM((rows, width), bf16),
            pltpu.VMEM((ndp, rows, depth), bf16),
            pltpu.VMEM((nz, rows, qcols + kvcols), f32),
            pltpu.VMEM((rows, HEAD_DIM), f32),
            pltpu.VMEM((rows, HEAD_DIM), f32),
            pltpu.VMEM((rows, rows + LANES), f32),
            pltpu.VMEM((KV_HEADS, rows, HEAD_DIM), bf16),
            pltpu.VMEM((KV_HEADS, rows, HEAD_DIM), bf16),
            pltpu.SemaphoreType.DMA((3,)),
            pltpu.SemaphoreType.DMA((4, nz)),
            pltpu.SemaphoreType.DMA(()),
            pltpu.SemaphoreType.DMA((ndp, nz, pieces)),
        ],
        compiler_params=pltpu.CompilerParams(
            collective_id=0, has_side_effects=True, vmem_limit_bytes=60 * 2**20),
        cost_estimate=pl.CostEstimate(
            flops=2 * rows * width * nz * (qcols + kvcols),
            bytes_accessed=2 * rows * width, transcendentals=0),
        name="gather_project_attend",
    )(hidden, q_weight, kv_weight, small)


def positions_of(segments):
    row_ids = jnp.arange(segments.shape[0], dtype=jnp.int32)
    before = jnp.concatenate([jnp.full((1,), -3, jnp.int32), segments[:-1]])
    starts = jnp.where(segments != before, row_ids, 0)
    return row_ids - lax.cummax(starts, axis=0)


def rotate(source, positions):
    half_dim = HEAD_DIM // 2
    frequency = jnp.exp(
        jnp.arange(half_dim, dtype=jnp.float32)
        * (-2.0 / HEAD_DIM)
        * jnp.log(jnp.float32(1000000.0))
    )
    angles = positions.astype(jnp.float32)[:, None] * frequency[None, :]
    cosine = jnp.cos(angles)[:, None, :]
    sine_part = jnp.sin(angles)[:, None, :]
    lower_half = source[..., :half_dim]
    second = source[..., half_dim:]
    return jnp.concatenate(
        [lower_half * cosine - second * sine_part, second * cosine + lower_half * sine_part],
        axis=-1,
    )


def normalize(hidden, norm_gain):
    as_float = hidden.astype(jnp.float32)
    mean_square = jnp.mean(as_float * as_float, axis=-1, keepdims=True)
    return (as_float * lax.rsqrt(mean_square + 1e-06) * norm_gain.astype(jnp.float32)).astype(
        jnp.bfloat16
    )


def windows(source, fill_value):
    block_count = source.shape[0] // BLOCK
    shaped = source.reshape((block_count, BLOCK) + source.shape[1:])
    padded = jnp.concatenate(
        [jnp.full((2,) + shaped.shape[1:], fill_value, source.dtype), shaped], axis=0
    )
    return jnp.concatenate(
        [padded[0:block_count], padded[1 : block_count + 1], padded[2 : block_count + 2]], axis=1
    )


def attend(queries, key_rows, values, segments):
    row_count = queries.shape[0]
    block_count = row_count // BLOCK
    group_size = HEADS // KV_HEADS
    row_ids = jnp.arange(row_count, dtype=jnp.int32)
    key_win = windows(key_rows, 0)
    value_win = windows(values, 0)
    seg_win = windows(segments, -2)
    row_win = windows(row_ids, -1)
    q_blocks = queries.reshape(block_count, BLOCK, KV_HEADS, group_size, HEAD_DIM)
    scores = jnp.einsum(
        "bqkgd,bskd->bkgqs", q_blocks, key_win, preferred_element_type=jnp.float32
    ) * HEAD_DIM ** (-0.5)
    q_seg = segments.reshape(block_count, BLOCK)
    q_row = row_ids.reshape(block_count, BLOCK)
    allowed = (
        (seg_win[:, None, :] == q_seg[:, :, None])
        & (row_win[:, None, :] <= q_row[:, :, None])
        & (q_seg[:, :, None] >= 0)
    )
    scores = jnp.where(allowed[:, None, None], scores, -1e30)
    row_max = jnp.max(scores, axis=-1, keepdims=True)
    exponents = jnp.exp(scores - row_max)
    probabilities = (exponents / jnp.sum(exponents, axis=-1, keepdims=True)).astype(jnp.bfloat16)
    context = jnp.einsum(
        "bkgqs,bskd->bqkgd", probabilities, value_win, preferred_element_type=jnp.float32
    )
    context = jnp.where((q_seg >= 0)[:, :, None, None, None], context, 0.0)
    return context.reshape(row_count, HEADS * HEAD_DIM).astype(jnp.bfloat16)


def project(row_input, positions, q_weight, kv_weight, q_bias, kv_bias):
    row_count = row_input.shape[0]
    q_rows_full, kv_rows_full = (
        lax.all_gather(q_weight, "fsdp", axis=1, tiled=True),
        lax.all_gather(kv_weight, "fsdp", axis=1, tiled=True),
    )

    def add_rows(piece_rows):
        return jnp.dot(row_input, piece_rows, preferred_element_type=jnp.float32)

    q_lin = add_rows(lax.all_gather(q_rows_full, "dp", axis=0, tiled=True))
    kv_lin = add_rows(lax.all_gather(kv_rows_full, "dp", axis=0, tiled=True))
    q_lin = q_lin + q_bias.astype(jnp.float32)
    kv_lin = kv_lin + kv_bias.astype(jnp.float32)
    split_at = KV_HEADS * HEAD_DIM
    queries = rotate(q_lin.reshape(row_count, HEADS, HEAD_DIM), positions).astype(jnp.bfloat16)
    key_rows = rotate(
        kv_lin[:, :split_at].reshape(row_count, KV_HEADS, HEAD_DIM), positions
    ).astype(jnp.bfloat16)
    values = kv_lin[:, split_at:].reshape(row_count, KV_HEADS, HEAD_DIM).astype(jnp.bfloat16)
    return (queries, key_rows, values)


def local(ndp, nz, hidden, norm_gain, q_weight, kv_weight, q_bias, kv_bias, segments):
    planes_fit = ndp == 2 * 2 * 2
    heads_fit = (
        nz == KV_HEADS
        and q_weight.shape[1] == HEADS // KV_HEADS * HEAD_DIM
        and kv_weight.shape[1] == 2 * HEAD_DIM
    )
    if planes_fit and heads_fit:
        return gather_project(
            ndp, nz, hidden, norm_gain, q_weight, kv_weight, q_bias, kv_bias, segments)
    normed = normalize(hidden, norm_gain)
    positions = positions_of(segments)
    queries, key_rows, values = project(normed, positions, q_weight, kv_weight, q_bias, kv_bias)
    return attend(queries, key_rows, values, segments)


def solution(mesh):
    in_specs = (
        P(("dp", "fsdp"), None),
        P(),
        P("dp", "fsdp"),
        P("dp", "fsdp"),
        P(),
        P(),
        P(("dp", "fsdp")),
    )
    out_specs = P(("dp", "fsdp"), None)
    return jax.shard_map(
        functools.partial(local, mesh.shape["dp"], mesh.shape["fsdp"]), mesh=mesh, in_specs=in_specs, out_specs=out_specs, check_vma=False)
```

```python
import functools

import jax
import jax.numpy as jnp
from jax import lax
from jax.experimental import pallas as pl
from jax.experimental.pallas import tpu as pltpu
from jax.sharding import PartitionSpec as P

HEADS = 20
KV_HEADS = 4
HEAD_DIM = 128
BLOCK = 128
LANES = 128
MESH = pl.DeviceIdType.MESH
TO_X, TO_Y, TO_UP, TO_DOWN = range(4)
OWN, VIA_X, VIA_Y, DIAG = range(4)
PIECE, LATE = range(2)


def gather_project_kernel(
    ndp, nz, pieces, late,
    hidden_ref, qw_ref, kvw_ref, gain_ref, qb_ref, kvb_ref, seg_ref,
    out_ref,
    wbuf, raw, normed, acc, cos_t, sin_t, mask_t, k_buf, v_buf, local_sem, send_sem, share_sem, recv_sem,
):
    rows, width = raw.shape
    depth, qcols = qw_ref.shape
    kvcols = kvw_ref.shape[1]
    cols = qcols + kvcols
    step = depth // pieces
    me = lax.axis_index("dp")
    z = lax.axis_index("fsdp")
    core = lax.rem(me, 2)
    x = lax.rem(me // 2, 2)
    y = me // 4
    sib = me + 1 - 2 * core
    xn = me + 2 - 4 * x
    yn = me + 4 - 8 * y
    dg = xn + yn - me
    source = [me, xn, yn, dg]

    own_q = pltpu.make_async_copy(qw_ref, wbuf.at[me, z, :, pl.ds(0, qcols)], local_sem.at[0])
    own_kv = pltpu.make_async_copy(kvw_ref, wbuf.at[me, z, :, pl.ds(qcols, kvcols)], local_sem.at[1])
    load = pltpu.make_async_copy(hidden_ref, raw, local_sem.at[2])
    own_q.start()
    own_kv.start()
    load.start()

    barrier = pltpu.get_barrier_semaphore()
    for other in (sib, xn, yn):
        pl.semaphore_signal(barrier, inc=1, device_id=(other, z), device_id_type=MESH)

    @pl.when(z > 0)
    def _():
        pl.semaphore_signal(barrier, inc=1, device_id=(me, z - 1), device_id_type=MESH)

    @pl.when(z < nz - 1)
    def _():
        pl.semaphore_signal(barrier, inc=1, device_id=(me, z + 1), device_id_type=MESH)

    pl.semaphore_wait(barrier, 3 + jnp.minimum(z, 1) + jnp.minimum(nz - 1 - z, 1))
    own_q.wait()
    own_kv.wait()

    def copy(way, src, plane, k):
        piece = wbuf.at[src, plane, pl.ds(pl.multiple_of(k * step, step), step), :]
        target = {
            TO_X: (xn, z), TO_Y: (yn, z), TO_UP: (me, z + 1), TO_DOWN: (me, z - 1),
        }[way]
        return pltpu.make_async_remote_copy(
            src_ref=piece, dst_ref=piece,
            send_sem=send_sem.at[way, plane],
            recv_sem=recv_sem.at[src, plane, k],
            device_id=target, device_id_type=MESH,
        )

    def shared(src, plane):
        shard = wbuf.at[src, plane]
        return pltpu.make_async_remote_copy(
            src_ref=shard, dst_ref=shard,
            send_sem=share_sem, recv_sem=recv_sem.at[src, plane, 0],
            device_id=(sib, z), device_id_type=MESH,
        )

    def ways(kind, rel, hop, sign):
        always = lambda k: True
        first = lambda k: lax.rem(k, 2) == 0
        second = lambda k: lax.rem(k, 2) == 1
        not_late = lambda k: k >= late
        up, down = (TO_UP, always, z < nz - 1), (TO_DOWN, always, z > 0)
        onward = up if sign > 0 else down
        if kind == LATE:
            return [up, down] if hop == 0 else [onward]
        if rel == OWN and hop == 0:
            return [up, down, (TO_X, always, True), (TO_Y, always, True)]
        if rel == OWN:
            return [onward, (TO_X, not_late, True), (TO_Y, not_late, True)]
        if rel == VIA_X:
            return [(TO_Y, first, True)]
        if rel == VIA_Y:
            return [(TO_X, second, True)]
        return []

    def place(hop, sign):
        plane = z - sign * hop
        return plane, (plane >= 0) & (plane < nz)

    def both(a, b):
        if a is True:
            return b
        return a if b is True else a & b

    def guarded(cond, do):
        if cond is True:
            do()
        else:
            pl.when(cond)(do)

    def span(kind, rel, hop):
        if kind == LATE:
            return 0, late
        return (0 if rel == OWN or hop == 0 else late), pieces

    def signs(hop):
        return (1,) if hop == 0 else (1, -1)

    def slots(kind, rels, hop):
        return [(kind, rel, hop, sign) for sign in signs(hop) for rel in rels]

    def arrive(kind, rel, hop, sign, k):
        plane, _ = place(hop, sign)
        src = source[rel]
        if hop > 0 or (rel != OWN and kind == PIECE):
            copy(TO_X, src, plane, k).wait_recv()
        for way, cond, reach in ways(kind, rel, hop, sign):
            guarded(both(cond(k), reach), lambda way=way: copy(way, src, plane, k).start())

    def each(todo, *extra):
        low = min(span(*slot[:3])[0] for slot in todo)
        high = max(span(*slot[:3])[1] for slot in todo)

        def body(k, carry):
            for kind, rel, hop, sign in todo:
                begin, _ = span(kind, rel, hop)
                cond = True if hop == 0 else place(hop, sign)[1]
                if begin > low:
                    cond = both(k >= begin, cond)
                guarded(cond, lambda slot=(kind, rel, hop, sign): arrive(*slot, k))
            for count, work in extra:
                per = -(-count // (high - low))

                def some(i, c, work=work):
                    work(i)
                    return c
                lax.fori_loop(jnp.minimum((k - low) * per, count),
                              jnp.minimum((k - low + 1) * per, count), some, 0)
            return carry
        lax.fori_loop(low, high, body, 0)

    def share(rels, hop):
        for sign in signs(hop):
            plane, ok = place(hop, sign)

            def send(plane=plane):
                for rel in rels:
                    shared(source[rel], plane).start()
            guarded(True if hop == 0 else ok, send)

    def multiply_one(hop, sign, rel, lane):
        plane, ok = place(hop, sign)
        base = me + lax.rem(rel, 2) * (xn - me) + (rel // 2) * (yn - me)
        src = base + lane * (sib - me)

        def run():
            @pl.when(lane == 1)
            def _():
                shared(src, plane).wait_recv()
            acc[plane] += jnp.dot(
                normed[src], wbuf[src, plane], preferred_element_type=jnp.float32
            )
        guarded(True if hop == 0 else ok, run)

    def shards(hop, low, high):
        ways_in, rels = len(signs(hop)), high - low

        def work(i):
            j = i // ways_in
            multiply_one(hop, 1 - 2 * lax.rem(i, ways_in), low + lax.rem(j, rels), j // rels)
        return ways_in * rels * 2, work

    def run_all(count, work):
        def body(i, carry):
            work(i)
            return carry
        lax.fori_loop(0, count, body, 0)

    each(slots(PIECE, [OWN], 0))
    share([OWN], 0)

    load.wait()
    group = 16

    gain = gain_ref[...].astype(jnp.float32).reshape(1, -1)

    def norm_rows(i, carry):
        at = pl.ds(pl.multiple_of(i * group, group), group)
        value = raw[at, :].astype(jnp.float32)
        mean = jnp.sum(value * value, axis=-1, keepdims=True) * (1.0 / width)
        scaled = value * lax.rsqrt(mean + 1e-06) * gain
        scaled = scaled.astype(jnp.bfloat16)
        for d in range(ndp):
            normed[d, at, :] = scaled[:, d * depth:(d + 1) * depth]
        return carry

    lax.fori_loop(0, rows // group, norm_rows, 0)
    for f in range(nz):
        acc[f, :, 0:qcols] = jnp.broadcast_to(
            qb_ref[f * qcols:(f + 1) * qcols].astype(jnp.float32).reshape(1, -1), (rows, qcols))
        acc[f, :, qcols:cols] = jnp.broadcast_to(
            kvb_ref[f * kvcols:(f + 1) * kvcols].astype(jnp.float32).reshape(1, -1), (rows, kvcols))
    each(slots(PIECE, [VIA_X, VIA_Y], 0) + slots(PIECE, [OWN], 1))
    share([VIA_X, VIA_Y], 0)
    share([OWN], 1)

    seg_row = seg_ref[...].astype(jnp.float32).reshape(1, -1)
    for b in range(rows // BLOCK):
        at = slice(b * BLOCK, (b + 1) * BLOCK)
        mine = jnp.transpose(jnp.broadcast_to(seg_row[:, at], (BLOCK, BLOCK)))[:, 0:1]
        ids = lax.broadcasted_iota(jnp.int32, (BLOCK, rows), 1).astype(jnp.float32)
        start = jnp.min(jnp.where(mine == seg_row, ids, float(rows)), axis=1, keepdims=True)
        here = (lax.broadcasted_iota(jnp.int32, (BLOCK, 1), 0) + b * BLOCK).astype(jnp.float32)
        position = here - start
        lane = lax.broadcasted_iota(jnp.int32, (BLOCK, HEAD_DIM), 1)
        half = HEAD_DIM // 2
        entry = jnp.where(lane < half, lane, lane - half).astype(jnp.float32)
        frequency = jnp.exp(entry * (-2.0 / HEAD_DIM) * jnp.log(jnp.float32(1000000.0)))
        angle = position * frequency
        cos_t[at, :] = jnp.cos(angle)
        sin_t[at, :] = jnp.where(lane < half, -1.0, 1.0) * jnp.sin(angle)
        allowed = (mine == seg_row) & (ids <= here) & (mine >= 0.0)
        mask_t[at, 0:rows] = jnp.where(allowed, 1.0, 0.0)
        mask_t[at, rows:] = jnp.broadcast_to(jnp.where(mine >= 0.0, 1.0, 0.0), (BLOCK, LANES))

    group = HEADS // KV_HEADS
    key_planes = nz // 2
    per_plane = kvcols // HEAD_DIM

    def rotated(value, at):
        return (value * cos_t[at, :] + pltpu.roll(value, HEAD_DIM // 2, 1) * sin_t[at, :]).astype(jnp.bfloat16)

    def prepare(g):
        at = slice(0, rows)
        lanes = pl.ds(pl.multiple_of(qcols + lax.rem(g, per_plane) * HEAD_DIM, HEAD_DIM), HEAD_DIM)
        k_buf[g] = rotated(acc[g // per_plane, :, lanes], at)
        v_buf[g] = acc[key_planes + g // per_plane, :, lanes].astype(jnp.bfloat16)

    scale = HEAD_DIM ** (-0.5) * 1.4426950408889634

    def attend_group(g):
        prepare(g)
        blocks = range(rows // BLOCK)
        scores, shares = [], []
        for b in blocks:
            at = slice(b * BLOCK, (b + 1) * BLOCK)
            seen = (b + 1) * BLOCK
            query = jnp.concatenate([
                rotated(acc[g, at, h * HEAD_DIM:(h + 1) * HEAD_DIM], at) for h in range(group)], axis=0)
            score = lax.dot_general(
                query, k_buf[g, 0:seen, :], (((1,), (1,)), ((), ())),
                preferred_element_type=jnp.float32).reshape(group, BLOCK, seen)
            scores.append(jnp.where(mask_t[at, 0:seen][None] > 0.5, score * scale, -1e30))
        tops = [jnp.max(score, axis=-1, keepdims=True) for score in scores]
        scores = [jnp.exp2(score - top) for score, top in zip(scores, tops)]
        sums = [jnp.sum(score, axis=-1, keepdims=True) for score in scores]
        for b in blocks:
            at = slice(b * BLOCK, (b + 1) * BLOCK)
            seen = (b + 1) * BLOCK
            share_of = mask_t[at, rows:rows + 1][None] / sums[b]
            p = (scores[b] * share_of).astype(jnp.bfloat16).reshape(group * BLOCK, seen)
            c = jnp.dot(p, v_buf[g, 0:seen, :], preferred_element_type=jnp.float32)
            for h in range(group):
                lanes = pl.ds(pl.multiple_of((g * group + h) * HEAD_DIM, HEAD_DIM), HEAD_DIM)
                out_ref[at, lanes] = c[h * BLOCK:(h + 1) * BLOCK].astype(out_ref.dtype)

    half_heads = KV_HEADS // 2
    near_first = (z // (nz // 2)) * half_heads
    far_first = half_heads - near_first

    each(slots(PIECE, [OWN], 2) + slots(PIECE, [DIAG], 0), shards(0, OWN, DIAG))
    each(slots(LATE, [VIA_X, VIA_Y, DIAG], 0))
    share([DIAG], 0)
    share([OWN], 2)
    each(slots(PIECE, [VIA_X, VIA_Y], 1), shards(0, DIAG, DIAG + 1), shards(1, OWN, VIA_X))
    each(slots(PIECE, [OWN], 3), shards(2, OWN, VIA_X))
    share([OWN], 3)
    each(slots(LATE, [VIA_X, VIA_Y, DIAG], 1))
    each(slots(PIECE, [VIA_X, VIA_Y], 2), shards(3, OWN, VIA_X))
    each(slots(LATE, [VIA_X, VIA_Y, DIAG], 2))
    share([VIA_X, VIA_Y], 2)
    each(slots(PIECE, [DIAG], 1))
    share([VIA_X, VIA_Y, DIAG], 1)
    each(slots(PIECE, [VIA_X, VIA_Y], 3), shards(1, VIA_X, DIAG + 1))
    run_all(*shards(2, VIA_X, DIAG))
    each(slots(PIECE, [DIAG], 2))
    share([DIAG], 2)
    each(slots(LATE, [VIA_X, VIA_Y, DIAG], 3))
    share([VIA_X, VIA_Y], 3)
    run_all(*shards(2, DIAG, DIAG + 1))
    run_all(half_heads, lambda i: attend_group(near_first + i))
    each(slots(PIECE, [DIAG], 3))
    share([DIAG], 3)
    run_all(*shards(3, VIA_X, DIAG))
    run_all(*shards(3, DIAG, DIAG + 1))
    run_all(half_heads, lambda i: attend_group(far_first + i))

    def sent(way, plane, count):
        some = wbuf.at[pl.ds(0, count), 0, pl.ds(0, step), :]
        pltpu.make_async_copy(some, some, send_sem.at[way, plane]).wait()

    def flat(plane, carry):
        @pl.when(plane == z)
        def _():
            sent(TO_X, plane, pieces + pieces // 2)
            sent(TO_Y, plane, pieces + (pieces + 1) // 2)

        @pl.when(plane != z)
        def _():
            odd = pieces // 2 - late // 2
            sent(TO_X, plane, pieces - late + odd)
            sent(TO_Y, plane, pieces - late + (pieces - late - odd))

        @pl.when((plane <= z) & (z < nz - 1))
        def _():
            sent(TO_UP, plane, pieces + 3 * late)

        @pl.when((plane >= z) & (z > 0))
        def _():
            sent(TO_DOWN, plane, pieces + 3 * late)
        return carry

    lax.fori_loop(0, nz, flat, 0)
    lane_shards = wbuf.at[pl.ds(0, ndp // 2)]
    pltpu.make_async_copy(lane_shards, lane_shards, share_sem).wait()


def gather_project(ndp, nz, hidden, norm_gain, q_weight, kv_weight, q_bias, kv_bias, segments):
    rows, width = hidden.shape
    depth, qcols = q_weight.shape
    kvcols = kv_weight.shape[1]
    pieces, late = 5, 1
    vmem = pl.BlockSpec(memory_space=pltpu.VMEM)
    hbm = pl.BlockSpec(memory_space=pl.ANY)
    bf16, f32 = jnp.bfloat16, jnp.float32
    return pl.pallas_call(
        functools.partial(gather_project_kernel, ndp, nz, pieces, late),
        out_shape=jax.ShapeDtypeStruct((rows, qcols * nz), bf16),
        in_specs=[hbm, hbm, hbm] + [vmem] * 4,
        out_specs=vmem,
        scratch_shapes=[
            pltpu.VMEM((ndp, nz, depth, qcols + kvcols), bf16),
            pltpu.VMEM((rows, width), bf16),
            pltpu.VMEM((ndp, rows, depth), bf16),
            pltpu.VMEM((nz, rows, qcols + kvcols), f32),
            pltpu.VMEM((rows, HEAD_DIM), f32),
            pltpu.VMEM((rows, HEAD_DIM), f32),
            pltpu.VMEM((rows, rows + LANES), f32),
            pltpu.VMEM((KV_HEADS, rows, HEAD_DIM), bf16),
            pltpu.VMEM((KV_HEADS, rows, HEAD_DIM), bf16),
            pltpu.SemaphoreType.DMA((3,)),
            pltpu.SemaphoreType.DMA((4, nz)),
            pltpu.SemaphoreType.DMA(()),
            pltpu.SemaphoreType.DMA((ndp, nz, pieces)),
        ],
        compiler_params=pltpu.CompilerParams(
            collective_id=0, has_side_effects=True, vmem_limit_bytes=60 * 2**20),
        cost_estimate=pl.CostEstimate(
            flops=2 * rows * width * nz * (qcols + kvcols),
            bytes_accessed=2 * rows * width, transcendentals=0),
        name="gather_project_attend",
    )(hidden, q_weight, kv_weight, norm_gain, q_bias, kv_bias, segments)


def positions_of(segments):
    row_ids = jnp.arange(segments.shape[0], dtype=jnp.int32)
    before = jnp.concatenate([jnp.full((1,), -3, jnp.int32), segments[:-1]])
    starts = jnp.where(segments != before, row_ids, 0)
    return row_ids - lax.cummax(starts, axis=0)


def rotate(source, positions):
    half_dim = HEAD_DIM // 2
    frequency = jnp.exp(
        jnp.arange(half_dim, dtype=jnp.float32)
        * (-2.0 / HEAD_DIM)
        * jnp.log(jnp.float32(1000000.0))
    )
    angles = positions.astype(jnp.float32)[:, None] * frequency[None, :]
    cosine = jnp.cos(angles)[:, None, :]
    sine_part = jnp.sin(angles)[:, None, :]
    lower_half = source[..., :half_dim]
    second = source[..., half_dim:]
    return jnp.concatenate(
        [lower_half * cosine - second * sine_part, second * cosine + lower_half * sine_part],
        axis=-1,
    )


def normalize(hidden, norm_gain):
    as_float = hidden.astype(jnp.float32)
    mean_square = jnp.mean(as_float * as_float, axis=-1, keepdims=True)
    return (as_float * lax.rsqrt(mean_square + 1e-06) * norm_gain.astype(jnp.float32)).astype(
        jnp.bfloat16
    )


def windows(source, fill_value):
    block_count = source.shape[0] // BLOCK
    shaped = source.reshape((block_count, BLOCK) + source.shape[1:])
    padded = jnp.concatenate(
        [jnp.full((2,) + shaped.shape[1:], fill_value, source.dtype), shaped], axis=0
    )
    return jnp.concatenate(
        [padded[0:block_count], padded[1 : block_count + 1], padded[2 : block_count + 2]], axis=1
    )


def attend(queries, key_rows, values, segments):
    row_count = queries.shape[0]
    block_count = row_count // BLOCK
    group_size = HEADS // KV_HEADS
    row_ids = jnp.arange(row_count, dtype=jnp.int32)
    key_win = windows(key_rows, 0)
    value_win = windows(values, 0)
    seg_win = windows(segments, -2)
    row_win = windows(row_ids, -1)
    q_blocks = queries.reshape(block_count, BLOCK, KV_HEADS, group_size, HEAD_DIM)
    scores = jnp.einsum(
        "bqkgd,bskd->bkgqs", q_blocks, key_win, preferred_element_type=jnp.float32
    ) * HEAD_DIM ** (-0.5)
    q_seg = segments.reshape(block_count, BLOCK)
    q_row = row_ids.reshape(block_count, BLOCK)
    allowed = (
        (seg_win[:, None, :] == q_seg[:, :, None])
        & (row_win[:, None, :] <= q_row[:, :, None])
        & (q_seg[:, :, None] >= 0)
    )
    scores = jnp.where(allowed[:, None, None], scores, -1e30)
    row_max = jnp.max(scores, axis=-1, keepdims=True)
    exponents = jnp.exp(scores - row_max)
    probabilities = (exponents / jnp.sum(exponents, axis=-1, keepdims=True)).astype(jnp.bfloat16)
    context = jnp.einsum(
        "bkgqs,bskd->bqkgd", probabilities, value_win, preferred_element_type=jnp.float32
    )
    context = jnp.where((q_seg >= 0)[:, :, None, None, None], context, 0.0)
    return context.reshape(row_count, HEADS * HEAD_DIM).astype(jnp.bfloat16)


def project(row_input, positions, q_weight, kv_weight, q_bias, kv_bias):
    row_count = row_input.shape[0]
    q_rows_full, kv_rows_full = (
        lax.all_gather(q_weight, "fsdp", axis=1, tiled=True),
        lax.all_gather(kv_weight, "fsdp", axis=1, tiled=True),
    )

    def add_rows(piece_rows):
        return jnp.dot(row_input, piece_rows, preferred_element_type=jnp.float32)

    q_lin = add_rows(lax.all_gather(q_rows_full, "dp", axis=0, tiled=True))
    kv_lin = add_rows(lax.all_gather(kv_rows_full, "dp", axis=0, tiled=True))
    q_lin = q_lin + q_bias.astype(jnp.float32)
    kv_lin = kv_lin + kv_bias.astype(jnp.float32)
    split_at = KV_HEADS * HEAD_DIM
    queries = rotate(q_lin.reshape(row_count, HEADS, HEAD_DIM), positions).astype(jnp.bfloat16)
    key_rows = rotate(
        kv_lin[:, :split_at].reshape(row_count, KV_HEADS, HEAD_DIM), positions
    ).astype(jnp.bfloat16)
    values = kv_lin[:, split_at:].reshape(row_count, KV_HEADS, HEAD_DIM).astype(jnp.bfloat16)
    return (queries, key_rows, values)


def local(ndp, nz, hidden, norm_gain, q_weight, kv_weight, q_bias, kv_bias, segments):
    planes_fit = ndp == 2 * 2 * 2
    heads_fit = (
        nz == KV_HEADS
        and q_weight.shape[1] == HEADS // KV_HEADS * HEAD_DIM
        and kv_weight.shape[1] == 2 * HEAD_DIM
    )
    if planes_fit and heads_fit:
        return gather_project(
            ndp, nz, hidden, norm_gain, q_weight, kv_weight, q_bias, kv_bias, segments)
    normed = normalize(hidden, norm_gain)
    positions = positions_of(segments)
    queries, key_rows, values = project(normed, positions, q_weight, kv_weight, q_bias, kv_bias)
    return attend(queries, key_rows, values, segments)


def solution(mesh):
    in_specs = (
        P(("dp", "fsdp"), None),
        P(),
        P("dp", "fsdp"),
        P("dp", "fsdp"),
        P(),
        P(),
        P(("dp", "fsdp")),
    )
    out_specs = P(("dp", "fsdp"), None)
    return jax.shard_map(
        functools.partial(local, mesh.shape["dp"], mesh.shape["fsdp"]), mesh=mesh, in_specs=in_specs, out_specs=out_specs, check_vma=False)
```

```python
import functools

import jax
import jax.numpy as jnp
from jax import lax
from jax.experimental import pallas as pl
from jax.experimental.pallas import tpu as pltpu
from jax.sharding import PartitionSpec as P

HEADS = 20
KV_HEADS = 4
HEAD_DIM = 128
BLOCK = 128
LANES = 128
MESH = pl.DeviceIdType.MESH
TO_X, TO_Y, TO_UP, TO_DOWN = range(4)
OWN, VIA_X, VIA_Y, DIAG = range(4)
PIECE, LATE = range(2)


def gather_project_kernel(
    ndp, nz, pieces, late,
    hidden_ref, qw_ref, kvw_ref, gain_ref, qb_ref, kvb_ref, seg_ref,
    out_ref,
    wbuf, raw, normed, acc, cos_t, sin_t, mask_t, k_buf, v_buf, local_sem, send_sem, share_sem, recv_sem,
):
    rows, width = raw.shape
    depth, qcols = qw_ref.shape
    kvcols = kvw_ref.shape[1]
    cols = qcols + kvcols
    step = depth // pieces
    me = lax.axis_index("dp")
    z = lax.axis_index("fsdp")
    core = lax.rem(me, 2)
    x = lax.rem(me // 2, 2)
    y = me // 4
    sib = me + 1 - 2 * core
    xn = me + 2 - 4 * x
    yn = me + 4 - 8 * y
    dg = xn + yn - me
    source = [me, xn, yn, dg]

    own_q = pltpu.make_async_copy(qw_ref, wbuf.at[me, z, :, pl.ds(0, qcols)], local_sem.at[0])
    own_kv = pltpu.make_async_copy(kvw_ref, wbuf.at[me, z, :, pl.ds(qcols, kvcols)], local_sem.at[1])
    load = pltpu.make_async_copy(hidden_ref, raw, local_sem.at[2])
    own_q.start()
    own_kv.start()
    load.start()

    barrier = pltpu.get_barrier_semaphore()
    for other in (sib, xn, yn):
        pl.semaphore_signal(barrier, inc=1, device_id=(other, z), device_id_type=MESH)

    @pl.when(z > 0)
    def _():
        pl.semaphore_signal(barrier, inc=1, device_id=(me, z - 1), device_id_type=MESH)

    @pl.when(z < nz - 1)
    def _():
        pl.semaphore_signal(barrier, inc=1, device_id=(me, z + 1), device_id_type=MESH)

    pl.semaphore_wait(barrier, 3 + jnp.minimum(z, 1) + jnp.minimum(nz - 1 - z, 1))
    own_q.wait()
    own_kv.wait()

    def copy(way, src, plane, k):
        piece = wbuf.at[src, plane, pl.ds(pl.multiple_of(k * step, step), step), :]
        target = {
            TO_X: (xn, z), TO_Y: (yn, z), TO_UP: (me, z + 1), TO_DOWN: (me, z - 1),
        }[way]
        return pltpu.make_async_remote_copy(
            src_ref=piece, dst_ref=piece,
            send_sem=send_sem.at[way, plane],
            recv_sem=recv_sem.at[src, plane, k],
            device_id=target, device_id_type=MESH,
        )

    def shared(src, plane):
        shard = wbuf.at[src, plane]
        return pltpu.make_async_remote_copy(
            src_ref=shard, dst_ref=shard,
            send_sem=share_sem, recv_sem=recv_sem.at[src, plane, 0],
            device_id=(sib, z), device_id_type=MESH,
        )

    def ways(kind, rel, hop, sign):
        always = lambda k: True
        first = lambda k: lax.rem(k, 2) == 0
        second = lambda k: lax.rem(k, 2) == 1
        not_late = lambda k: k >= late
        up, down = (TO_UP, always, z < nz - 1), (TO_DOWN, always, z > 0)
        onward = up if sign > 0 else down
        if kind == LATE:
            return [up, down] if hop == 0 else [onward]
        if rel == OWN and hop == 0:
            return [up, down, (TO_X, always, True), (TO_Y, always, True)]
        if rel == OWN:
            return [onward, (TO_X, not_late, True), (TO_Y, not_late, True)]
        if rel == VIA_X:
            return [(TO_Y, first, True)]
        if rel == VIA_Y:
            return [(TO_X, second, True)]
        return []

    def place(hop, sign):
        plane = z - sign * hop
        return plane, (plane >= 0) & (plane < nz)

    def both(a, b):
        if a is True:
            return b
        return a if b is True else a & b

    def guarded(cond, do):
        if cond is True:
            do()
        else:
            pl.when(cond)(do)

    def span(kind, rel, hop):
        if kind == LATE:
            return 0, late
        return (0 if rel == OWN or hop == 0 else late), pieces

    def signs(hop):
        return (1,) if hop == 0 else (1, -1)

    def slots(kind, rels, hop):
        return [(kind, rel, hop, sign) for sign in signs(hop) for rel in rels]

    def arrive(kind, rel, hop, sign, k):
        plane, _ = place(hop, sign)
        src = source[rel]
        if hop > 0 or (rel != OWN and kind == PIECE):
            copy(TO_X, src, plane, k).wait_recv()
        for way, cond, reach in ways(kind, rel, hop, sign):
            guarded(both(cond(k), reach), lambda way=way: copy(way, src, plane, k).start())

    def each(todo, *extra):
        low = min(span(*slot[:3])[0] for slot in todo)
        high = max(span(*slot[:3])[1] for slot in todo)

        def body(k, carry):
            for kind, rel, hop, sign in todo:
                begin, _ = span(kind, rel, hop)
                cond = True if hop == 0 else place(hop, sign)[1]
                if begin > low:
                    cond = both(k >= begin, cond)
                guarded(cond, lambda slot=(kind, rel, hop, sign): arrive(*slot, k))
            for count, work in extra:
                per = -(-count // (high - low))

                def some(i, c, work=work):
                    work(i)
                    return c
                lax.fori_loop(jnp.minimum((k - low) * per, count),
                              jnp.minimum((k - low + 1) * per, count), some, 0)
            return carry
        lax.fori_loop(low, high, body, 0)

    def share(rels, hop):
        for sign in signs(hop):
            plane, ok = place(hop, sign)

            def send(plane=plane):
                for rel in rels:
                    shared(source[rel], plane).start()
            guarded(True if hop == 0 else ok, send)

    def multiply_one(hop, sign, rel, lane):
        plane, ok = place(hop, sign)
        base = me + lax.rem(rel, 2) * (xn - me) + (rel // 2) * (yn - me)
        src = base + lane * (sib - me)

        def run():
            @pl.when(lane == 1)
            def _():
                shared(src, plane).wait_recv()
            acc[plane] += jnp.dot(
                normed[src], wbuf[src, plane], preferred_element_type=jnp.float32
            )
        guarded(True if hop == 0 else ok, run)

    def shards(hop, low, high):
        ways_in, rels = len(signs(hop)), high - low

        def work(i):
            j = i // ways_in
            multiply_one(hop, 1 - 2 * lax.rem(i, ways_in), low + lax.rem(j, rels), j // rels)
        return ways_in * rels * 2, work

    def run_all(count, work):
        def body(i, carry):
            work(i)
            return carry
        lax.fori_loop(0, count, body, 0)

    each(slots(PIECE, [OWN], 0))
    share([OWN], 0)

    load.wait()
    group = 16

    gain = gain_ref[...].astype(jnp.float32).reshape(1, -1)

    def norm_rows(i, carry):
        at = pl.ds(pl.multiple_of(i * group, group), group)
        value = raw[at, :].astype(jnp.float32)
        mean = jnp.sum(value * value, axis=-1, keepdims=True) * (1.0 / width)
        scaled = value * lax.rsqrt(mean + 1e-06) * gain
        scaled = scaled.astype(jnp.bfloat16)
        for d in range(ndp):
            normed[d, at, :] = scaled[:, d * depth:(d + 1) * depth]
        return carry

    lax.fori_loop(0, rows // group, norm_rows, 0)
    for f in range(nz):
        acc[f, :, 0:qcols] = jnp.broadcast_to(
            qb_ref[f * qcols:(f + 1) * qcols].astype(jnp.float32).reshape(1, -1), (rows, qcols))
        acc[f, :, qcols:cols] = jnp.broadcast_to(
            kvb_ref[f * kvcols:(f + 1) * kvcols].astype(jnp.float32).reshape(1, -1), (rows, kvcols))
    each(slots(PIECE, [VIA_X, VIA_Y], 0) + slots(PIECE, [OWN], 1))
    share([VIA_X, VIA_Y], 0)
    share([OWN], 1)

    seg_row = seg_ref[...].astype(jnp.float32).reshape(1, -1)
    for b in range(rows // BLOCK):
        at = slice(b * BLOCK, (b + 1) * BLOCK)
        mine = jnp.transpose(jnp.broadcast_to(seg_row[:, at], (BLOCK, BLOCK)))[:, 0:1]
        ids = lax.broadcasted_iota(jnp.int32, (BLOCK, rows), 1).astype(jnp.float32)
        start = jnp.min(jnp.where(mine == seg_row, ids, float(rows)), axis=1, keepdims=True)
        here = (lax.broadcasted_iota(jnp.int32, (BLOCK, 1), 0) + b * BLOCK).astype(jnp.float32)
        position = here - start
        lane = lax.broadcasted_iota(jnp.int32, (BLOCK, HEAD_DIM), 1)
        half = HEAD_DIM // 2
        entry = jnp.where(lane < half, lane, lane - half).astype(jnp.float32)
        frequency = jnp.exp(entry * (-2.0 / HEAD_DIM) * jnp.log(jnp.float32(1000000.0)))
        angle = position * frequency
        cos_t[at, :] = jnp.cos(angle)
        sin_t[at, :] = jnp.where(lane < half, -1.0, 1.0) * jnp.sin(angle)
        allowed = (mine == seg_row) & (ids <= here) & (mine >= 0.0)
        mask_t[at, 0:rows] = jnp.where(allowed, 1.0, 0.0)
        mask_t[at, rows:] = jnp.broadcast_to(jnp.where(mine >= 0.0, 1.0, 0.0), (BLOCK, LANES))

    group = HEADS // KV_HEADS
    key_planes = nz // 2
    per_plane = kvcols // HEAD_DIM

    def rotated(value, at):
        return (value * cos_t[at, :] + pltpu.roll(value, HEAD_DIM // 2, 1) * sin_t[at, :]).astype(jnp.bfloat16)

    def prepare(g):
        at = slice(0, rows)
        lanes = pl.ds(pl.multiple_of(qcols + lax.rem(g, per_plane) * HEAD_DIM, HEAD_DIM), HEAD_DIM)
        k_buf[g] = rotated(acc[g // per_plane, :, lanes], at)
        v_buf[g] = acc[key_planes + g // per_plane, :, lanes].astype(jnp.bfloat16)

    scale = HEAD_DIM ** (-0.5) * 1.4426950408889634

    def attend_group(g):
        prepare(g)
        blocks = range(rows // BLOCK)
        scores, shares = [], []
        for b in blocks:
            at = slice(b * BLOCK, (b + 1) * BLOCK)
            seen = (b + 1) * BLOCK
            query = jnp.concatenate([
                rotated(acc[g, at, h * HEAD_DIM:(h + 1) * HEAD_DIM], at) for h in range(group)], axis=0)
            score = lax.dot_general(
                query, k_buf[g, 0:seen, :], (((1,), (1,)), ((), ())),
                preferred_element_type=jnp.float32).reshape(group, BLOCK, seen)
            scores.append(jnp.where(mask_t[at, 0:seen][None] > 0.5, score * scale, -1e30))
        tops = [jnp.max(score, axis=-1, keepdims=True) for score in scores]
        scores = [jnp.exp2(score - top) for score, top in zip(scores, tops)]
        sums = [jnp.sum(score, axis=-1, keepdims=True) for score in scores]
        for b in blocks:
            at = slice(b * BLOCK, (b + 1) * BLOCK)
            seen = (b + 1) * BLOCK
            share_of = mask_t[at, rows:rows + 1][None] / sums[b]
            p = (scores[b] * share_of).astype(jnp.bfloat16).reshape(group * BLOCK, seen)
            c = jnp.dot(p, v_buf[g, 0:seen, :], preferred_element_type=jnp.float32)
            for h in range(group):
                lanes = pl.ds(pl.multiple_of((g * group + h) * HEAD_DIM, HEAD_DIM), HEAD_DIM)
                out_ref[at, lanes] = c[h * BLOCK:(h + 1) * BLOCK].astype(out_ref.dtype)

    half_heads = KV_HEADS // 2
    near_first = (z // (nz // 2)) * half_heads
    far_first = half_heads - near_first

    each(slots(PIECE, [OWN], 2) + slots(PIECE, [DIAG], 0), shards(0, OWN, DIAG))
    each(slots(LATE, [VIA_X, VIA_Y, DIAG], 0))
    share([DIAG], 0)
    share([OWN], 2)
    each(slots(PIECE, [VIA_X, VIA_Y], 1), shards(0, DIAG, DIAG + 1), shards(1, OWN, VIA_X))
    each(slots(PIECE, [OWN], 3), shards(2, OWN, VIA_X))
    share([OWN], 3)
    each(slots(LATE, [VIA_X, VIA_Y, DIAG], 1))
    share([VIA_X, VIA_Y], 1)
    each(slots(PIECE, [VIA_X, VIA_Y], 2), shards(3, OWN, VIA_X), shards(1, VIA_X, DIAG))
    each(slots(LATE, [VIA_X, VIA_Y, DIAG], 2))
    share([VIA_X, VIA_Y], 2)

    inner = (z > 0) & (z < nz - 1)
    count, second_hop = shards(2, VIA_X, DIAG)

    @pl.when(inner)
    def _():
        run_all(count, second_hop)

    def second_hop_at_end(i):
        @pl.when(jnp.logical_not(inner))
        def _():
            second_hop(i)

    each(slots(PIECE, [DIAG], 1))
    share([DIAG], 1)
    each(slots(PIECE, [VIA_X, VIA_Y], 3), shards(1, DIAG, DIAG + 1), (count, second_hop_at_end))

    @pl.when(inner)
    def _():
        run_all(half_heads, lambda i: attend_group(near_first + i))

    each(slots(PIECE, [DIAG], 2))
    share([DIAG], 2)
    each(slots(LATE, [VIA_X, VIA_Y, DIAG], 3))
    share([VIA_X, VIA_Y], 3)
    run_all(*shards(2, DIAG, DIAG + 1))

    @pl.when(jnp.logical_not(inner))
    def _():
        run_all(half_heads, lambda i: attend_group(near_first + i))

    each(slots(PIECE, [DIAG], 3))
    share([DIAG], 3)
    run_all(*shards(3, VIA_X, DIAG))
    run_all(*shards(3, DIAG, DIAG + 1))
    run_all(half_heads, lambda i: attend_group(far_first + i))

    def sent(way, plane, count):
        some = wbuf.at[pl.ds(0, count), 0, pl.ds(0, step), :]
        pltpu.make_async_copy(some, some, send_sem.at[way, plane]).wait()

    def flat(plane, carry):
        @pl.when(plane == z)
        def _():
            sent(TO_X, plane, pieces + pieces // 2)
            sent(TO_Y, plane, pieces + (pieces + 1) // 2)

        @pl.when(plane != z)
        def _():
            odd = pieces // 2 - late // 2
            sent(TO_X, plane, pieces - late + odd)
            sent(TO_Y, plane, pieces - late + (pieces - late - odd))

        @pl.when((plane <= z) & (z < nz - 1))
        def _():
            sent(TO_UP, plane, pieces + 3 * late)

        @pl.when((plane >= z) & (z > 0))
        def _():
            sent(TO_DOWN, plane, pieces + 3 * late)
        return carry

    lax.fori_loop(0, nz, flat, 0)
    lane_shards = wbuf.at[pl.ds(0, ndp // 2)]
    pltpu.make_async_copy(lane_shards, lane_shards, share_sem).wait()


def gather_project(ndp, nz, hidden, norm_gain, q_weight, kv_weight, q_bias, kv_bias, segments):
    rows, width = hidden.shape
    depth, qcols = q_weight.shape
    kvcols = kv_weight.shape[1]
    pieces, late = 5, 1
    vmem = pl.BlockSpec(memory_space=pltpu.VMEM)
    hbm = pl.BlockSpec(memory_space=pl.ANY)
    bf16, f32 = jnp.bfloat16, jnp.float32
    return pl.pallas_call(
        functools.partial(gather_project_kernel, ndp, nz, pieces, late),
        out_shape=jax.ShapeDtypeStruct((rows, qcols * nz), bf16),
        in_specs=[hbm, hbm, hbm] + [vmem] * 4,
        out_specs=vmem,
        scratch_shapes=[
            pltpu.VMEM((ndp, nz, depth, qcols + kvcols), bf16),
            pltpu.VMEM((rows, width), bf16),
            pltpu.VMEM((ndp, rows, depth), bf16),
            pltpu.VMEM((nz, rows, qcols + kvcols), f32),
            pltpu.VMEM((rows, HEAD_DIM), f32),
            pltpu.VMEM((rows, HEAD_DIM), f32),
            pltpu.VMEM((rows, rows + LANES), f32),
            pltpu.VMEM((KV_HEADS, rows, HEAD_DIM), bf16),
            pltpu.VMEM((KV_HEADS, rows, HEAD_DIM), bf16),
            pltpu.SemaphoreType.DMA((3,)),
            pltpu.SemaphoreType.DMA((4, nz)),
            pltpu.SemaphoreType.DMA(()),
            pltpu.SemaphoreType.DMA((ndp, nz, pieces)),
        ],
        compiler_params=pltpu.CompilerParams(
            collective_id=0, has_side_effects=True, vmem_limit_bytes=60 * 2**20),
        cost_estimate=pl.CostEstimate(
            flops=2 * rows * width * nz * (qcols + kvcols),
            bytes_accessed=2 * rows * width, transcendentals=0),
        name="gather_project_attend",
    )(hidden, q_weight, kv_weight, norm_gain, q_bias, kv_bias, segments)


def positions_of(segments):
    row_ids = jnp.arange(segments.shape[0], dtype=jnp.int32)
    before = jnp.concatenate([jnp.full((1,), -3, jnp.int32), segments[:-1]])
    starts = jnp.where(segments != before, row_ids, 0)
    return row_ids - lax.cummax(starts, axis=0)


def rotate(source, positions):
    half_dim = HEAD_DIM // 2
    frequency = jnp.exp(
        jnp.arange(half_dim, dtype=jnp.float32)
        * (-2.0 / HEAD_DIM)
        * jnp.log(jnp.float32(1000000.0))
    )
    angles = positions.astype(jnp.float32)[:, None] * frequency[None, :]
    cosine = jnp.cos(angles)[:, None, :]
    sine_part = jnp.sin(angles)[:, None, :]
    lower_half = source[..., :half_dim]
    second = source[..., half_dim:]
    return jnp.concatenate(
        [lower_half * cosine - second * sine_part, second * cosine + lower_half * sine_part],
        axis=-1,
    )


def normalize(hidden, norm_gain):
    as_float = hidden.astype(jnp.float32)
    mean_square = jnp.mean(as_float * as_float, axis=-1, keepdims=True)
    return (as_float * lax.rsqrt(mean_square + 1e-06) * norm_gain.astype(jnp.float32)).astype(
        jnp.bfloat16
    )


def windows(source, fill_value):
    block_count = source.shape[0] // BLOCK
    shaped = source.reshape((block_count, BLOCK) + source.shape[1:])
    padded = jnp.concatenate(
        [jnp.full((2,) + shaped.shape[1:], fill_value, source.dtype), shaped], axis=0
    )
    return jnp.concatenate(
        [padded[0:block_count], padded[1 : block_count + 1], padded[2 : block_count + 2]], axis=1
    )


def attend(queries, key_rows, values, segments):
    row_count = queries.shape[0]
    block_count = row_count // BLOCK
    group_size = HEADS // KV_HEADS
    row_ids = jnp.arange(row_count, dtype=jnp.int32)
    key_win = windows(key_rows, 0)
    value_win = windows(values, 0)
    seg_win = windows(segments, -2)
    row_win = windows(row_ids, -1)
    q_blocks = queries.reshape(block_count, BLOCK, KV_HEADS, group_size, HEAD_DIM)
    scores = jnp.einsum(
        "bqkgd,bskd->bkgqs", q_blocks, key_win, preferred_element_type=jnp.float32
    ) * HEAD_DIM ** (-0.5)
    q_seg = segments.reshape(block_count, BLOCK)
    q_row = row_ids.reshape(block_count, BLOCK)
    allowed = (
        (seg_win[:, None, :] == q_seg[:, :, None])
        & (row_win[:, None, :] <= q_row[:, :, None])
        & (q_seg[:, :, None] >= 0)
    )
    scores = jnp.where(allowed[:, None, None], scores, -1e30)
    row_max = jnp.max(scores, axis=-1, keepdims=True)
    exponents = jnp.exp(scores - row_max)
    probabilities = (exponents / jnp.sum(exponents, axis=-1, keepdims=True)).astype(jnp.bfloat16)
    context = jnp.einsum(
        "bkgqs,bskd->bqkgd", probabilities, value_win, preferred_element_type=jnp.float32
    )
    context = jnp.where((q_seg >= 0)[:, :, None, None, None], context, 0.0)
    return context.reshape(row_count, HEADS * HEAD_DIM).astype(jnp.bfloat16)


def project(row_input, positions, q_weight, kv_weight, q_bias, kv_bias):
    row_count = row_input.shape[0]
    q_rows_full, kv_rows_full = (
        lax.all_gather(q_weight, "fsdp", axis=1, tiled=True),
        lax.all_gather(kv_weight, "fsdp", axis=1, tiled=True),
    )

    def add_rows(piece_rows):
        return jnp.dot(row_input, piece_rows, preferred_element_type=jnp.float32)

    q_lin = add_rows(lax.all_gather(q_rows_full, "dp", axis=0, tiled=True))
    kv_lin = add_rows(lax.all_gather(kv_rows_full, "dp", axis=0, tiled=True))
    q_lin = q_lin + q_bias.astype(jnp.float32)
    kv_lin = kv_lin + kv_bias.astype(jnp.float32)
    split_at = KV_HEADS * HEAD_DIM
    queries = rotate(q_lin.reshape(row_count, HEADS, HEAD_DIM), positions).astype(jnp.bfloat16)
    key_rows = rotate(
        kv_lin[:, :split_at].reshape(row_count, KV_HEADS, HEAD_DIM), positions
    ).astype(jnp.bfloat16)
    values = kv_lin[:, split_at:].reshape(row_count, KV_HEADS, HEAD_DIM).astype(jnp.bfloat16)
    return (queries, key_rows, values)


def local(ndp, nz, hidden, norm_gain, q_weight, kv_weight, q_bias, kv_bias, segments):
    planes_fit = ndp == 2 * 2 * 2
    heads_fit = (
        nz == KV_HEADS
        and q_weight.shape[1] == HEADS // KV_HEADS * HEAD_DIM
        and kv_weight.shape[1] == 2 * HEAD_DIM
    )
    if planes_fit and heads_fit:
        return gather_project(
            ndp, nz, hidden, norm_gain, q_weight, kv_weight, q_bias, kv_bias, segments)
    normed = normalize(hidden, norm_gain)
    positions = positions_of(segments)
    queries, key_rows, values = project(normed, positions, q_weight, kv_weight, q_bias, kv_bias)
    return attend(queries, key_rows, values, segments)


def solution(mesh):
    in_specs = (
        P(("dp", "fsdp"), None),
        P(),
        P("dp", "fsdp"),
        P("dp", "fsdp"),
        P(),
        P(),
        P(("dp", "fsdp")),
    )
    out_specs = P(("dp", "fsdp"), None)
    return jax.shard_map(
        functools.partial(local, mesh.shape["dp"], mesh.shape["fsdp"]), mesh=mesh, in_specs=in_specs, out_specs=out_specs, check_vma=False)
```

```python
import functools

import jax
import jax.numpy as jnp
from jax import lax
from jax.experimental import pallas as pl
from jax.experimental.pallas import tpu as pltpu
from jax.sharding import PartitionSpec as P

HEADS = 20
KV_HEADS = 4
HEAD_DIM = 128
BLOCK = 128
LANES = 128
MESH = pl.DeviceIdType.MESH
TO_X, TO_Y, TO_UP, TO_DOWN = range(4)
OWN, VIA_X, VIA_Y, DIAG = range(4)
PIECE, LATE = range(2)


def gather_project_kernel(
    ndp, nz, pieces, late,
    hidden_ref, qw_ref, kvw_ref, gain_ref, qb_ref, kvb_ref, seg_ref,
    out_ref,
    wbuf, raw, normed, acc, cos_t, sin_t, mask_t, k_buf, v_buf, local_sem, send_sem, share_sem, recv_sem,
):
    rows, width = raw.shape
    depth, qcols = qw_ref.shape
    kvcols = kvw_ref.shape[1]
    cols = qcols + kvcols
    step = depth // pieces
    me = lax.axis_index("dp")
    z = lax.axis_index("fsdp")
    core = lax.rem(me, 2)
    x = lax.rem(me // 2, 2)
    y = me // 4
    sib = me + 1 - 2 * core
    xn = me + 2 - 4 * x
    yn = me + 4 - 8 * y
    dg = xn + yn - me
    source = [me, xn, yn, dg]

    own_q = pltpu.make_async_copy(qw_ref, wbuf.at[me, z, :, pl.ds(0, qcols)], local_sem.at[0])
    own_kv = pltpu.make_async_copy(kvw_ref, wbuf.at[me, z, :, pl.ds(qcols, kvcols)], local_sem.at[1])
    load = pltpu.make_async_copy(hidden_ref, raw, local_sem.at[2])
    own_q.start()
    own_kv.start()
    load.start()

    barrier = pltpu.get_barrier_semaphore()
    for other in (sib, xn, yn):
        pl.semaphore_signal(barrier, inc=1, device_id=(other, z), device_id_type=MESH)

    @pl.when(z > 0)
    def _():
        pl.semaphore_signal(barrier, inc=1, device_id=(me, z - 1), device_id_type=MESH)

    @pl.when(z < nz - 1)
    def _():
        pl.semaphore_signal(barrier, inc=1, device_id=(me, z + 1), device_id_type=MESH)

    pl.semaphore_wait(barrier, 3 + jnp.minimum(z, 1) + jnp.minimum(nz - 1 - z, 1))
    own_q.wait()
    own_kv.wait()

    def copy(way, src, plane, k):
        piece = wbuf.at[src, plane, pl.ds(pl.multiple_of(k * step, step), step), :]
        target = {
            TO_X: (xn, z), TO_Y: (yn, z), TO_UP: (me, z + 1), TO_DOWN: (me, z - 1),
        }[way]
        return pltpu.make_async_remote_copy(
            src_ref=piece, dst_ref=piece,
            send_sem=send_sem.at[way, plane],
            recv_sem=recv_sem.at[src, plane, k],
            device_id=target, device_id_type=MESH,
        )

    def shared(src, plane):
        shard = wbuf.at[src, plane]
        return pltpu.make_async_remote_copy(
            src_ref=shard, dst_ref=shard,
            send_sem=share_sem, recv_sem=recv_sem.at[src, plane, 0],
            device_id=(sib, z), device_id_type=MESH,
        )

    def ways(kind, rel, hop, sign):
        always = lambda k: True
        first = lambda k: lax.rem(k, 2) == 0
        second = lambda k: lax.rem(k, 2) == 1
        not_late = lambda k: k >= late
        up, down = (TO_UP, always, z < nz - 1), (TO_DOWN, always, z > 0)
        onward = up if sign > 0 else down
        if kind == LATE:
            return [up, down] if hop == 0 else [onward]
        if rel == OWN and hop == 0:
            return [up, down, (TO_X, always, True), (TO_Y, always, True)]
        if rel == OWN:
            return [onward, (TO_X, not_late, True), (TO_Y, not_late, True)]
        if rel == VIA_X:
            return [(TO_Y, first, True)]
        if rel == VIA_Y:
            return [(TO_X, second, True)]
        return []

    def place(hop, sign):
        plane = z - sign * hop
        return plane, (plane >= 0) & (plane < nz)

    def both(a, b):
        if a is True:
            return b
        return a if b is True else a & b

    def guarded(cond, do):
        if cond is True:
            do()
        else:
            pl.when(cond)(do)

    def span(kind, rel, hop):
        if kind == LATE:
            return 0, late
        return (0 if rel == OWN or hop == 0 else late), pieces

    def signs(hop):
        return (1,) if hop == 0 else (1, -1)

    def slots(kind, rels, hop):
        return [(kind, rel, hop, sign) for sign in signs(hop) for rel in rels]

    def arrive(kind, rel, hop, sign, k):
        plane, _ = place(hop, sign)
        src = source[rel]
        if hop > 0 or (rel != OWN and kind == PIECE):
            copy(TO_X, src, plane, k).wait_recv()
        for way, cond, reach in ways(kind, rel, hop, sign):
            guarded(both(cond(k), reach), lambda way=way: copy(way, src, plane, k).start())

    def each(todo, *extra):
        low = min(span(*slot[:3])[0] for slot in todo)
        high = max(span(*slot[:3])[1] for slot in todo)

        def body(k, carry):
            for kind, rel, hop, sign in todo:
                begin, _ = span(kind, rel, hop)
                cond = True if hop == 0 else place(hop, sign)[1]
                if begin > low:
                    cond = both(k >= begin, cond)
                guarded(cond, lambda slot=(kind, rel, hop, sign): arrive(*slot, k))
            for count, work in extra:
                per = -(-count // (high - low))

                def some(i, c, work=work):
                    work(i)
                    return c
                lax.fori_loop(jnp.minimum((k - low) * per, count),
                              jnp.minimum((k - low + 1) * per, count), some, 0)
            return carry
        lax.fori_loop(low, high, body, 0)

    def share(rels, hop):
        for sign in signs(hop):
            plane, ok = place(hop, sign)

            def send(plane=plane):
                for rel in rels:
                    shared(source[rel], plane).start()
            guarded(True if hop == 0 else ok, send)

    def multiply_one(hop, sign, rel, lane):
        plane, ok = place(hop, sign)
        base = me + lax.rem(rel, 2) * (xn - me) + (rel // 2) * (yn - me)
        src = base + lane * (sib - me)

        def run():
            @pl.when(lane == 1)
            def _():
                shared(src, plane).wait_recv()
            acc[plane] += jnp.dot(
                normed[src], wbuf[src, plane], preferred_element_type=jnp.float32
            )
        guarded(True if hop == 0 else ok, run)

    def shards(hop, low, high):
        ways_in, rels = len(signs(hop)), high - low

        def work(i):
            j = i // ways_in
            multiply_one(hop, 1 - 2 * lax.rem(i, ways_in), low + lax.rem(j, rels), j // rels)
        return ways_in * rels * 2, work

    def run_all(count, work):
        def body(i, carry):
            work(i)
            return carry
        lax.fori_loop(0, count, body, 0)

    each(slots(PIECE, [OWN], 0))
    share([OWN], 0)

    load.wait()
    group = 16

    gain = gain_ref[...].astype(jnp.float32).reshape(1, -1)

    def norm_rows(i, carry):
        at = pl.ds(pl.multiple_of(i * group, group), group)
        value = raw[at, :].astype(jnp.float32)
        mean = jnp.sum(value * value, axis=-1, keepdims=True) * (1.0 / width)
        scaled = value * lax.rsqrt(mean + 1e-06) * gain
        scaled = scaled.astype(jnp.bfloat16)
        for d in range(ndp):
            normed[d, at, :] = scaled[:, d * depth:(d + 1) * depth]
        return carry

    lax.fori_loop(0, rows // group, norm_rows, 0)
    for f in range(nz):
        acc[f, :, 0:qcols] = jnp.broadcast_to(
            qb_ref[f * qcols:(f + 1) * qcols].astype(jnp.float32).reshape(1, -1), (rows, qcols))
        acc[f, :, qcols:cols] = jnp.broadcast_to(
            kvb_ref[f * kvcols:(f + 1) * kvcols].astype(jnp.float32).reshape(1, -1), (rows, kvcols))
    each(slots(PIECE, [VIA_X, VIA_Y], 0) + slots(PIECE, [OWN], 1))
    share([VIA_X, VIA_Y], 0)
    share([OWN], 1)

    seg_row = seg_ref[...].astype(jnp.float32).reshape(1, -1)
    for b in range(rows // BLOCK):
        at = slice(b * BLOCK, (b + 1) * BLOCK)
        mine = jnp.transpose(jnp.broadcast_to(seg_row[:, at], (BLOCK, BLOCK)))[:, 0:1]
        ids = lax.broadcasted_iota(jnp.int32, (BLOCK, rows), 1).astype(jnp.float32)
        start = jnp.min(jnp.where(mine == seg_row, ids, float(rows)), axis=1, keepdims=True)
        here = (lax.broadcasted_iota(jnp.int32, (BLOCK, 1), 0) + b * BLOCK).astype(jnp.float32)
        position = here - start
        lane = lax.broadcasted_iota(jnp.int32, (BLOCK, HEAD_DIM), 1)
        half = HEAD_DIM // 2
        entry = jnp.where(lane < half, lane, lane - half).astype(jnp.float32)
        frequency = jnp.exp(entry * (-2.0 / HEAD_DIM) * jnp.log(jnp.float32(1000000.0)))
        angle = position * frequency
        cos_t[at, :] = jnp.cos(angle)
        sin_t[at, :] = jnp.where(lane < half, -1.0, 1.0) * jnp.sin(angle)
        allowed = (mine == seg_row) & (ids <= here) & (mine >= 0.0)
        mask_t[at, 0:rows] = jnp.where(allowed, 1.0, 0.0)
        mask_t[at, rows:] = jnp.broadcast_to(jnp.where(mine >= 0.0, 1.0, 0.0), (BLOCK, LANES))

    group = HEADS // KV_HEADS
    key_planes = nz // 2
    per_plane = kvcols // HEAD_DIM

    def rotated(value, at):
        return (value * cos_t[at, :] + pltpu.roll(value, HEAD_DIM // 2, 1) * sin_t[at, :]).astype(jnp.bfloat16)

    def prepare(g):
        at = slice(0, rows)
        lanes = pl.ds(pl.multiple_of(qcols + lax.rem(g, per_plane) * HEAD_DIM, HEAD_DIM), HEAD_DIM)
        k_buf[g] = rotated(acc[g // per_plane, :, lanes], at)
        v_buf[g] = acc[key_planes + g // per_plane, :, lanes].astype(jnp.bfloat16)

    scale = HEAD_DIM ** (-0.5) * 1.4426950408889634

    def attend_group(g):
        prepare(g)
        blocks = range(rows // BLOCK)
        scores, shares = [], []
        for b in blocks:
            at = slice(b * BLOCK, (b + 1) * BLOCK)
            seen = (b + 1) * BLOCK
            query = jnp.concatenate([
                rotated(acc[g, at, h * HEAD_DIM:(h + 1) * HEAD_DIM], at) for h in range(group)], axis=0)
            score = lax.dot_general(
                query, k_buf[g, 0:seen, :], (((1,), (1,)), ((), ())),
                preferred_element_type=jnp.float32).reshape(group, BLOCK, seen)
            scores.append(jnp.where(mask_t[at, 0:seen][None] > 0.5, score * scale, -1e30))
        tops = [jnp.max(score, axis=-1, keepdims=True) for score in scores]
        scores = [jnp.exp2(score - top) for score, top in zip(scores, tops)]
        sums = [jnp.sum(score, axis=-1, keepdims=True) for score in scores]
        for b in blocks:
            at = slice(b * BLOCK, (b + 1) * BLOCK)
            seen = (b + 1) * BLOCK
            share_of = mask_t[at, rows:rows + 1][None] / sums[b]
            p = (scores[b] * share_of).astype(jnp.bfloat16).reshape(group * BLOCK, seen)
            c = jnp.dot(p, v_buf[g, 0:seen, :], preferred_element_type=jnp.float32)
            for h in range(group):
                lanes = pl.ds(pl.multiple_of((g * group + h) * HEAD_DIM, HEAD_DIM), HEAD_DIM)
                out_ref[at, lanes] = c[h * BLOCK:(h + 1) * BLOCK].astype(out_ref.dtype)

    half_heads = KV_HEADS // 2
    near_first = (z // (nz // 2)) * half_heads
    far_first = half_heads - near_first

    each(slots(PIECE, [OWN], 2) + slots(PIECE, [DIAG], 0), shards(0, OWN, DIAG))
    each(slots(LATE, [VIA_X, VIA_Y, DIAG], 0))
    share([DIAG], 0)
    share([OWN], 2)
    each(slots(PIECE, [VIA_X, VIA_Y], 1), shards(0, DIAG, DIAG + 1), shards(1, OWN, VIA_X))
    each(slots(PIECE, [OWN], 3), shards(2, OWN, VIA_X))
    share([OWN], 3)
    each(slots(LATE, [VIA_X, VIA_Y, DIAG], 1))
    share([VIA_X, VIA_Y], 1)
    each(slots(PIECE, [VIA_X, VIA_Y], 2), shards(3, OWN, VIA_X), shards(1, VIA_X, DIAG))
    each(slots(LATE, [VIA_X, VIA_Y, DIAG], 2))
    share([VIA_X, VIA_Y], 2)

    inner = (z > 0) & (z < nz - 1)
    count, second_hop = shards(2, VIA_X, DIAG)

    @pl.when(inner)
    def _():
        run_all(count, second_hop)

    def second_hop_at_end(i):
        @pl.when(jnp.logical_not(inner))
        def _():
            second_hop(i)

    each(slots(PIECE, [DIAG], 1))
    share([DIAG], 1)
    each(slots(PIECE, [VIA_X, VIA_Y], 3), shards(1, DIAG, DIAG + 1), (count, second_hop_at_end))

    @pl.when(inner)
    def _():
        run_all(half_heads, lambda i: attend_group(near_first + i))

    each(slots(PIECE, [DIAG], 2))
    share([DIAG], 2)
    each(slots(LATE, [VIA_X, VIA_Y, DIAG], 3))
    share([VIA_X, VIA_Y], 3)
    run_all(*shards(2, DIAG, DIAG + 1))

    @pl.when(jnp.logical_not(inner))
    def _():
        run_all(half_heads, lambda i: attend_group(near_first + i))

    each(slots(PIECE, [DIAG], 3))
    share([DIAG], 3)
    run_all(*shards(3, VIA_X, DIAG))
    run_all(*shards(3, DIAG, DIAG + 1))
    run_all(half_heads, lambda i: attend_group(far_first + i))

    def sent(way, plane, count):
        total = count * step
        parts = next(p for p in range(1, ndp + 1) if total % (p * 16) == 0 and total // p <= depth)
        some = wbuf.at[pl.ds(0, parts), 0, pl.ds(0, total // parts), :]
        pltpu.make_async_copy(some, some, send_sem.at[way, plane]).wait()

    def flat(plane, carry):
        @pl.when(plane == z)
        def _():
            sent(TO_X, plane, pieces + pieces // 2)
            sent(TO_Y, plane, pieces + (pieces + 1) // 2)

        @pl.when(plane != z)
        def _():
            odd = pieces // 2 - late // 2
            sent(TO_X, plane, pieces - late + odd)
            sent(TO_Y, plane, pieces - late + (pieces - late - odd))

        @pl.when((plane <= z) & (z < nz - 1))
        def _():
            sent(TO_UP, plane, pieces + 3 * late)

        @pl.when((plane >= z) & (z > 0))
        def _():
            sent(TO_DOWN, plane, pieces + 3 * late)
        return carry

    lax.fori_loop(0, nz, flat, 0)
    lane_shards = wbuf.at[pl.ds(0, ndp // 2)]
    pltpu.make_async_copy(lane_shards, lane_shards, share_sem).wait()


def gather_project(ndp, nz, hidden, norm_gain, q_weight, kv_weight, q_bias, kv_bias, segments):
    rows, width = hidden.shape
    depth, qcols = q_weight.shape
    kvcols = kv_weight.shape[1]
    pieces, late = 10, 2
    vmem = pl.BlockSpec(memory_space=pltpu.VMEM)
    hbm = pl.BlockSpec(memory_space=pl.ANY)
    bf16, f32 = jnp.bfloat16, jnp.float32
    return pl.pallas_call(
        functools.partial(gather_project_kernel, ndp, nz, pieces, late),
        out_shape=jax.ShapeDtypeStruct((rows, qcols * nz), bf16),
        in_specs=[hbm, hbm, hbm] + [vmem] * 4,
        out_specs=vmem,
        scratch_shapes=[
            pltpu.VMEM((ndp, nz, depth, qcols + kvcols), bf16),
            pltpu.VMEM((rows, width), bf16),
            pltpu.VMEM((ndp, rows, depth), bf16),
            pltpu.VMEM((nz, rows, qcols + kvcols), f32),
            pltpu.VMEM((rows, HEAD_DIM), f32),
            pltpu.VMEM((rows, HEAD_DIM), f32),
            pltpu.VMEM((rows, rows + LANES), f32),
            pltpu.VMEM((KV_HEADS, rows, HEAD_DIM), bf16),
            pltpu.VMEM((KV_HEADS, rows, HEAD_DIM), bf16),
            pltpu.SemaphoreType.DMA((3,)),
            pltpu.SemaphoreType.DMA((4, nz)),
            pltpu.SemaphoreType.DMA(()),
            pltpu.SemaphoreType.DMA((ndp, nz, pieces)),
        ],
        compiler_params=pltpu.CompilerParams(
            collective_id=0, has_side_effects=True, vmem_limit_bytes=60 * 2**20),
        cost_estimate=pl.CostEstimate(
            flops=2 * rows * width * nz * (qcols + kvcols),
            bytes_accessed=2 * rows * width, transcendentals=0),
        name="gather_project_attend",
    )(hidden, q_weight, kv_weight, norm_gain, q_bias, kv_bias, segments)


def positions_of(segments):
    row_ids = jnp.arange(segments.shape[0], dtype=jnp.int32)
    before = jnp.concatenate([jnp.full((1,), -3, jnp.int32), segments[:-1]])
    starts = jnp.where(segments != before, row_ids, 0)
    return row_ids - lax.cummax(starts, axis=0)


def rotate(source, positions):
    half_dim = HEAD_DIM // 2
    frequency = jnp.exp(
        jnp.arange(half_dim, dtype=jnp.float32)
        * (-2.0 / HEAD_DIM)
        * jnp.log(jnp.float32(1000000.0))
    )
    angles = positions.astype(jnp.float32)[:, None] * frequency[None, :]
    cosine = jnp.cos(angles)[:, None, :]
    sine_part = jnp.sin(angles)[:, None, :]
    lower_half = source[..., :half_dim]
    second = source[..., half_dim:]
    return jnp.concatenate(
        [lower_half * cosine - second * sine_part, second * cosine + lower_half * sine_part],
        axis=-1,
    )


def normalize(hidden, norm_gain):
    as_float = hidden.astype(jnp.float32)
    mean_square = jnp.mean(as_float * as_float, axis=-1, keepdims=True)
    return (as_float * lax.rsqrt(mean_square + 1e-06) * norm_gain.astype(jnp.float32)).astype(
        jnp.bfloat16
    )


def windows(source, fill_value):
    block_count = source.shape[0] // BLOCK
    shaped = source.reshape((block_count, BLOCK) + source.shape[1:])
    padded = jnp.concatenate(
        [jnp.full((2,) + shaped.shape[1:], fill_value, source.dtype), shaped], axis=0
    )
    return jnp.concatenate(
        [padded[0:block_count], padded[1 : block_count + 1], padded[2 : block_count + 2]], axis=1
    )


def attend(queries, key_rows, values, segments):
    row_count = queries.shape[0]
    block_count = row_count // BLOCK
    group_size = HEADS // KV_HEADS
    row_ids = jnp.arange(row_count, dtype=jnp.int32)
    key_win = windows(key_rows, 0)
    value_win = windows(values, 0)
    seg_win = windows(segments, -2)
    row_win = windows(row_ids, -1)
    q_blocks = queries.reshape(block_count, BLOCK, KV_HEADS, group_size, HEAD_DIM)
    scores = jnp.einsum(
        "bqkgd,bskd->bkgqs", q_blocks, key_win, preferred_element_type=jnp.float32
    ) * HEAD_DIM ** (-0.5)
    q_seg = segments.reshape(block_count, BLOCK)
    q_row = row_ids.reshape(block_count, BLOCK)
    allowed = (
        (seg_win[:, None, :] == q_seg[:, :, None])
        & (row_win[:, None, :] <= q_row[:, :, None])
        & (q_seg[:, :, None] >= 0)
    )
    scores = jnp.where(allowed[:, None, None], scores, -1e30)
    row_max = jnp.max(scores, axis=-1, keepdims=True)
    exponents = jnp.exp(scores - row_max)
    probabilities = (exponents / jnp.sum(exponents, axis=-1, keepdims=True)).astype(jnp.bfloat16)
    context = jnp.einsum(
        "bkgqs,bskd->bqkgd", probabilities, value_win, preferred_element_type=jnp.float32
    )
    context = jnp.where((q_seg >= 0)[:, :, None, None, None], context, 0.0)
    return context.reshape(row_count, HEADS * HEAD_DIM).astype(jnp.bfloat16)


def project(row_input, positions, q_weight, kv_weight, q_bias, kv_bias):
    row_count = row_input.shape[0]
    q_rows_full, kv_rows_full = (
        lax.all_gather(q_weight, "fsdp", axis=1, tiled=True),
        lax.all_gather(kv_weight, "fsdp", axis=1, tiled=True),
    )

    def add_rows(piece_rows):
        return jnp.dot(row_input, piece_rows, preferred_element_type=jnp.float32)

    q_lin = add_rows(lax.all_gather(q_rows_full, "dp", axis=0, tiled=True))
    kv_lin = add_rows(lax.all_gather(kv_rows_full, "dp", axis=0, tiled=True))
    q_lin = q_lin + q_bias.astype(jnp.float32)
    kv_lin = kv_lin + kv_bias.astype(jnp.float32)
    split_at = KV_HEADS * HEAD_DIM
    queries = rotate(q_lin.reshape(row_count, HEADS, HEAD_DIM), positions).astype(jnp.bfloat16)
    key_rows = rotate(
        kv_lin[:, :split_at].reshape(row_count, KV_HEADS, HEAD_DIM), positions
    ).astype(jnp.bfloat16)
    values = kv_lin[:, split_at:].reshape(row_count, KV_HEADS, HEAD_DIM).astype(jnp.bfloat16)
    return (queries, key_rows, values)


def local(ndp, nz, hidden, norm_gain, q_weight, kv_weight, q_bias, kv_bias, segments):
    planes_fit = ndp == 2 * 2 * 2
    heads_fit = (
        nz == KV_HEADS
        and q_weight.shape[1] == HEADS // KV_HEADS * HEAD_DIM
        and kv_weight.shape[1] == 2 * HEAD_DIM
    )
    if planes_fit and heads_fit:
        return gather_project(
            ndp, nz, hidden, norm_gain, q_weight, kv_weight, q_bias, kv_bias, segments)
    normed = normalize(hidden, norm_gain)
    positions = positions_of(segments)
    queries, key_rows, values = project(normed, positions, q_weight, kv_weight, q_bias, kv_bias)
    return attend(queries, key_rows, values, segments)


def solution(mesh):
    in_specs = (
        P(("dp", "fsdp"), None),
        P(),
        P("dp", "fsdp"),
        P("dp", "fsdp"),
        P(),
        P(),
        P(("dp", "fsdp")),
    )
    out_specs = P(("dp", "fsdp"), None)
    return jax.shard_map(
        functools.partial(local, mesh.shape["dp"], mesh.shape["fsdp"]), mesh=mesh, in_specs=in_specs, out_specs=out_specs, check_vma=False)
```

```python
import functools

import jax
import jax.numpy as jnp
from jax import lax
from jax.experimental import pallas as pl
from jax.experimental.pallas import tpu as pltpu
from jax.sharding import PartitionSpec as P

HEADS = 20
KV_HEADS = 4
HEAD_DIM = 128
BLOCK = 128
LANES = 128
MESH = pl.DeviceIdType.MESH
TO_X, TO_Y, TO_UP, TO_DOWN = range(4)
OWN, VIA_X, VIA_Y, DIAG = range(4)
PIECE, LATE = range(2)


def gather_project_kernel(
    ndp, nz, pieces, late,
    hidden_ref, qw_ref, kvw_ref, gain_ref, qb_ref, kvb_ref, seg_ref,
    out_ref,
    wbuf, raw, normed, acc, cos_t, sin_t, mask_t, k_buf, v_buf, local_sem, out_sem, send_sem, share_sem, recv_sem,
):
    rows, width = raw.shape
    depth, qcols = qw_ref.shape
    kvcols = kvw_ref.shape[1]
    cols = qcols + kvcols
    step = depth // pieces
    me = lax.axis_index("dp")
    z = lax.axis_index("fsdp")
    core = lax.rem(me, 2)
    x = lax.rem(me // 2, 2)
    y = me // 4
    sib = me + 1 - 2 * core
    xn = me + 2 - 4 * x
    yn = me + 4 - 8 * y
    dg = xn + yn - me
    source = [me, xn, yn, dg]

    own_q = pltpu.make_async_copy(qw_ref, wbuf.at[me, z, :, pl.ds(0, qcols)], local_sem.at[0])
    own_kv = pltpu.make_async_copy(kvw_ref, wbuf.at[me, z, :, pl.ds(qcols, kvcols)], local_sem.at[1])
    load = pltpu.make_async_copy(hidden_ref, raw, local_sem.at[2])
    own_q.start()
    own_kv.start()
    load.start()

    barrier = pltpu.get_barrier_semaphore()
    for other in (sib, xn, yn):
        pl.semaphore_signal(barrier, inc=1, device_id=(other, z), device_id_type=MESH)

    @pl.when(z > 0)
    def _():
        pl.semaphore_signal(barrier, inc=1, device_id=(me, z - 1), device_id_type=MESH)

    @pl.when(z < nz - 1)
    def _():
        pl.semaphore_signal(barrier, inc=1, device_id=(me, z + 1), device_id_type=MESH)

    pl.semaphore_wait(barrier, 3 + jnp.minimum(z, 1) + jnp.minimum(nz - 1 - z, 1))
    own_q.wait()
    own_kv.wait()

    def copy(way, src, plane, k):
        piece = wbuf.at[src, plane, pl.ds(pl.multiple_of(k * step, step), step), :]
        target = {
            TO_X: (xn, z), TO_Y: (yn, z), TO_UP: (me, z + 1), TO_DOWN: (me, z - 1),
        }[way]
        return pltpu.make_async_remote_copy(
            src_ref=piece, dst_ref=piece,
            send_sem=send_sem.at[way, plane],
            recv_sem=recv_sem.at[src, plane, k],
            device_id=target, device_id_type=MESH,
        )

    def shared(src, plane):
        shard = wbuf.at[src, plane]
        return pltpu.make_async_remote_copy(
            src_ref=shard, dst_ref=shard,
            send_sem=share_sem, recv_sem=recv_sem.at[src, plane, 0],
            device_id=(sib, z), device_id_type=MESH,
        )

    def ways(kind, rel, hop, sign):
        always = lambda k: True
        first = lambda k: lax.rem(k, 2) == 0
        second = lambda k: lax.rem(k, 2) == 1
        not_late = lambda k: k >= late
        up, down = (TO_UP, always, z < nz - 1), (TO_DOWN, always, z > 0)
        onward = up if sign > 0 else down
        if kind == LATE:
            return [up, down] if hop == 0 else [onward]
        if rel == OWN and hop == 0:
            return [up, down, (TO_X, always, True), (TO_Y, always, True)]
        if rel == OWN:
            return [onward, (TO_X, not_late, True), (TO_Y, not_late, True)]
        if rel == VIA_X:
            return [(TO_Y, first, True)]
        if rel == VIA_Y:
            return [(TO_X, second, True)]
        return []

    def place(hop, sign):
        plane = z - sign * hop
        return plane, (plane >= 0) & (plane < nz)

    def both(a, b):
        if a is True:
            return b
        return a if b is True else a & b

    def guarded(cond, do):
        if cond is True:
            do()
        else:
            pl.when(cond)(do)

    def span(kind, rel, hop):
        if kind == LATE:
            return 0, late
        return (0 if rel == OWN or hop == 0 else late), pieces

    def signs(hop):
        return (1,) if hop == 0 else (1, -1)

    def slots(kind, rels, hop):
        return [(kind, rel, hop, sign) for sign in signs(hop) for rel in rels]

    def arrive(kind, rel, hop, sign, k):
        plane, _ = place(hop, sign)
        src = source[rel]
        if hop > 0 or (rel != OWN and kind == PIECE):
            copy(TO_X, src, plane, k).wait_recv()
        for way, cond, reach in ways(kind, rel, hop, sign):
            guarded(both(cond(k), reach), lambda way=way: copy(way, src, plane, k).start())

    def each(todo, *extra):
        low = min(span(*slot[:3])[0] for slot in todo)
        high = max(span(*slot[:3])[1] for slot in todo)

        def body(k, carry):
            for kind, rel, hop, sign in todo:
                begin, _ = span(kind, rel, hop)
                cond = True if hop == 0 else place(hop, sign)[1]
                if begin > low:
                    cond = both(k >= begin, cond)
                guarded(cond, lambda slot=(kind, rel, hop, sign): arrive(*slot, k))
            for count, work in extra:
                per = -(-count // (high - low))

                def some(i, c, work=work):
                    work(i)
                    return c
                lax.fori_loop(jnp.minimum((k - low) * per, count),
                              jnp.minimum((k - low + 1) * per, count), some, 0)
            return carry
        lax.fori_loop(low, high, body, 0)

    def share(rels, hop):
        for sign in signs(hop):
            plane, ok = place(hop, sign)

            def send(plane=plane):
                for rel in rels:
                    shared(source[rel], plane).start()
            guarded(True if hop == 0 else ok, send)

    def multiply_one(hop, sign, rel, lane):
        plane, ok = place(hop, sign)
        base = me + lax.rem(rel, 2) * (xn - me) + (rel // 2) * (yn - me)
        src = base + lane * (sib - me)

        def run():
            @pl.when(lane == 1)
            def _():
                shared(src, plane).wait_recv()
            acc[plane] += jnp.dot(
                normed[src], wbuf[src, plane], preferred_element_type=jnp.float32
            )
        guarded(True if hop == 0 else ok, run)

    def shards(hop, low, high):
        ways_in, rels = len(signs(hop)), high - low

        def work(i):
            j = i // ways_in
            multiply_one(hop, 1 - 2 * lax.rem(i, ways_in), low + lax.rem(j, rels), j // rels)
        return ways_in * rels * 2, work

    def run_all(count, work):
        def body(i, carry):
            work(i)
            return carry
        lax.fori_loop(0, count, body, 0)

    each(slots(PIECE, [OWN], 0))
    share([OWN], 0)

    load.wait()
    group = 16

    gain = gain_ref[...].astype(jnp.float32).reshape(1, -1)

    def norm_rows(i, carry):
        at = pl.ds(pl.multiple_of(i * group, group), group)
        value = raw[at, :].astype(jnp.float32)
        mean = jnp.sum(value * value, axis=-1, keepdims=True) * (1.0 / width)
        scaled = value * lax.rsqrt(mean + 1e-06) * gain
        scaled = scaled.astype(jnp.bfloat16)
        for d in range(ndp):
            normed[d, at, :] = scaled[:, d * depth:(d + 1) * depth]
        return carry

    lax.fori_loop(0, rows // group, norm_rows, 0)
    for f in range(nz):
        acc[f, :, 0:qcols] = jnp.broadcast_to(
            qb_ref[f * qcols:(f + 1) * qcols].astype(jnp.float32).reshape(1, -1), (rows, qcols))
        acc[f, :, qcols:cols] = jnp.broadcast_to(
            kvb_ref[f * kvcols:(f + 1) * kvcols].astype(jnp.float32).reshape(1, -1), (rows, kvcols))
    each(slots(PIECE, [VIA_X, VIA_Y], 0) + slots(PIECE, [OWN], 1))
    share([VIA_X, VIA_Y], 0)
    share([OWN], 1)

    seg_row = seg_ref[...].astype(jnp.float32).reshape(1, -1)
    for b in range(rows // BLOCK):
        at = slice(b * BLOCK, (b + 1) * BLOCK)
        mine = jnp.transpose(jnp.broadcast_to(seg_row[:, at], (BLOCK, BLOCK)))[:, 0:1]
        ids = lax.broadcasted_iota(jnp.int32, (BLOCK, rows), 1).astype(jnp.float32)
        start = jnp.min(jnp.where(mine == seg_row, ids, float(rows)), axis=1, keepdims=True)
        here = (lax.broadcasted_iota(jnp.int32, (BLOCK, 1), 0) + b * BLOCK).astype(jnp.float32)
        position = here - start
        lane = lax.broadcasted_iota(jnp.int32, (BLOCK, HEAD_DIM), 1)
        half = HEAD_DIM // 2
        entry = jnp.where(lane < half, lane, lane - half).astype(jnp.float32)
        frequency = jnp.exp(entry * (-2.0 / HEAD_DIM) * jnp.log(jnp.float32(1000000.0)))
        angle = position * frequency
        cos_t[at, :] = jnp.cos(angle)
        sin_t[at, :] = jnp.where(lane < half, -1.0, 1.0) * jnp.sin(angle)
        allowed = (mine == seg_row) & (ids <= here) & (mine >= 0.0)
        mask_t[at, 0:rows] = jnp.where(allowed, 1.0, 0.0)
        mask_t[at, rows:] = jnp.broadcast_to(jnp.where(mine >= 0.0, 1.0, 0.0), (BLOCK, LANES))

    group = HEADS // KV_HEADS
    key_planes = nz // 2
    per_plane = kvcols // HEAD_DIM

    def rotated(value, at):
        return (value * cos_t[at, :] + pltpu.roll(value, HEAD_DIM // 2, 1) * sin_t[at, :]).astype(jnp.bfloat16)

    def prepare(g):
        at = slice(0, rows)
        lanes = pl.ds(pl.multiple_of(qcols + lax.rem(g, per_plane) * HEAD_DIM, HEAD_DIM), HEAD_DIM)
        k_buf[g] = rotated(acc[g // per_plane, :, lanes], at)
        v_buf[g] = acc[key_planes + g // per_plane, :, lanes].astype(jnp.bfloat16)

    scale = HEAD_DIM ** (-0.5) * 1.4426950408889634

    def result(g):
        lanes = pl.ds(pl.multiple_of(g * group * HEAD_DIM, HEAD_DIM), group * HEAD_DIM)
        return pltpu.make_async_copy(raw.at[:, lanes], out_ref.at[:, lanes], out_sem.at[g])

    def attend_group(g):
        prepare(g)
        blocks = range(rows // BLOCK)
        scores, shares = [], []
        for b in blocks:
            at = slice(b * BLOCK, (b + 1) * BLOCK)
            seen = (b + 1) * BLOCK
            query = jnp.concatenate([
                rotated(acc[g, at, h * HEAD_DIM:(h + 1) * HEAD_DIM], at) for h in range(group)], axis=0)
            score = lax.dot_general(
                query, k_buf[g, 0:seen, :], (((1,), (1,)), ((), ())),
                preferred_element_type=jnp.float32).reshape(group, BLOCK, seen)
            scores.append(jnp.where(mask_t[at, 0:seen][None] > 0.5, score * scale, -1e30))
        tops = [jnp.max(score, axis=-1, keepdims=True) for score in scores]
        scores = [jnp.exp2(score - top) for score, top in zip(scores, tops)]
        sums = [jnp.sum(score, axis=-1, keepdims=True) for score in scores]
        for b in blocks:
            at = slice(b * BLOCK, (b + 1) * BLOCK)
            seen = (b + 1) * BLOCK
            share_of = mask_t[at, rows:rows + 1][None] / sums[b]
            p = (scores[b] * share_of).astype(jnp.bfloat16).reshape(group * BLOCK, seen)
            c = jnp.dot(p, v_buf[g, 0:seen, :], preferred_element_type=jnp.float32)
            for h in range(group):
                lanes = pl.ds(pl.multiple_of((g * group + h) * HEAD_DIM, HEAD_DIM), HEAD_DIM)
                raw[at, lanes] = c[h * BLOCK:(h + 1) * BLOCK].astype(raw.dtype)
        result(g).start()

    half_heads = KV_HEADS // 2
    near_first = (z // (nz // 2)) * half_heads
    far_first = half_heads - near_first

    each(slots(PIECE, [OWN], 2) + slots(PIECE, [DIAG], 0), shards(0, OWN, DIAG))
    each(slots(LATE, [VIA_X, VIA_Y, DIAG], 0))
    share([DIAG], 0)
    share([OWN], 2)
    each(slots(PIECE, [VIA_X, VIA_Y], 1), shards(0, DIAG, DIAG + 1), shards(1, OWN, VIA_X))
    each(slots(PIECE, [OWN], 3), shards(2, OWN, VIA_X))
    share([OWN], 3)
    each(slots(LATE, [VIA_X, VIA_Y, DIAG], 1))
    share([VIA_X, VIA_Y], 1)
    each(slots(PIECE, [VIA_X, VIA_Y], 2), shards(3, OWN, VIA_X), shards(1, VIA_X, DIAG))
    each(slots(LATE, [VIA_X, VIA_Y, DIAG], 2))
    share([VIA_X, VIA_Y], 2)

    inner = (z > 0) & (z < nz - 1)
    count, second_hop = shards(2, VIA_X, DIAG)

    @pl.when(inner)
    def _():
        run_all(count, second_hop)

    def second_hop_at_end(i):
        @pl.when(jnp.logical_not(inner))
        def _():
            second_hop(i)

    each(slots(PIECE, [DIAG], 1))
    share([DIAG], 1)
    each(slots(PIECE, [VIA_X, VIA_Y], 3), shards(1, DIAG, DIAG + 1), (count, second_hop_at_end))

    @pl.when(inner)
    def _():
        run_all(half_heads, lambda i: attend_group(near_first + i))

    each(slots(PIECE, [DIAG], 2))
    share([DIAG], 2)
    each(slots(LATE, [VIA_X, VIA_Y, DIAG], 3))
    share([VIA_X, VIA_Y], 3)
    run_all(*shards(2, DIAG, DIAG + 1))

    @pl.when(jnp.logical_not(inner))
    def _():
        run_all(half_heads, lambda i: attend_group(near_first + i))

    each(slots(PIECE, [DIAG], 3))
    share([DIAG], 3)
    run_all(*shards(3, VIA_X, DIAG))
    run_all(*shards(3, DIAG, DIAG + 1))
    run_all(half_heads, lambda i: attend_group(far_first + i))

    def sent(way, plane, count):
        total = count * step
        parts = next(p for p in range(1, ndp + 1) if total % (p * 16) == 0 and total // p <= depth)
        some = wbuf.at[pl.ds(0, parts), 0, pl.ds(0, total // parts), :]
        pltpu.make_async_copy(some, some, send_sem.at[way, plane]).wait()

    def flat(plane, carry):
        @pl.when(plane == z)
        def _():
            sent(TO_X, plane, pieces + pieces // 2)
            sent(TO_Y, plane, pieces + (pieces + 1) // 2)

        @pl.when(plane != z)
        def _():
            odd = pieces // 2 - late // 2
            sent(TO_X, plane, pieces - late + odd)
            sent(TO_Y, plane, pieces - late + (pieces - late - odd))

        @pl.when((plane <= z) & (z < nz - 1))
        def _():
            sent(TO_UP, plane, pieces + 3 * late)

        @pl.when((plane >= z) & (z > 0))
        def _():
            sent(TO_DOWN, plane, pieces + 3 * late)
        return carry

    lax.fori_loop(0, nz, flat, 0)
    run_all(KV_HEADS, lambda g: result(g).wait())
    lane_shards = wbuf.at[pl.ds(0, ndp // 2)]
    pltpu.make_async_copy(lane_shards, lane_shards, share_sem).wait()


def gather_project(ndp, nz, hidden, norm_gain, q_weight, kv_weight, q_bias, kv_bias, segments):
    rows, width = hidden.shape
    depth, qcols = q_weight.shape
    kvcols = kv_weight.shape[1]
    pieces, late = 10, 2
    vmem = pl.BlockSpec(memory_space=pltpu.VMEM)
    hbm = pl.BlockSpec(memory_space=pl.ANY)
    bf16, f32 = jnp.bfloat16, jnp.float32
    return pl.pallas_call(
        functools.partial(gather_project_kernel, ndp, nz, pieces, late),
        out_shape=jax.ShapeDtypeStruct((rows, qcols * nz), bf16),
        in_specs=[hbm, hbm, hbm] + [vmem] * 4,
        out_specs=hbm,
        scratch_shapes=[
            pltpu.VMEM((ndp, nz, depth, qcols + kvcols), bf16),
            pltpu.VMEM((rows, width), bf16),
            pltpu.VMEM((ndp, rows, depth), bf16),
            pltpu.VMEM((nz, rows, qcols + kvcols), f32),
            pltpu.VMEM((rows, HEAD_DIM), f32),
            pltpu.VMEM((rows, HEAD_DIM), f32),
            pltpu.VMEM((rows, rows + LANES), f32),
            pltpu.VMEM((KV_HEADS, rows, HEAD_DIM), bf16),
            pltpu.VMEM((KV_HEADS, rows, HEAD_DIM), bf16),
            pltpu.SemaphoreType.DMA((3,)),
            pltpu.SemaphoreType.DMA((KV_HEADS,)),
            pltpu.SemaphoreType.DMA((4, nz)),
            pltpu.SemaphoreType.DMA(()),
            pltpu.SemaphoreType.DMA((ndp, nz, pieces)),
        ],
        compiler_params=pltpu.CompilerParams(
            collective_id=0, has_side_effects=True, vmem_limit_bytes=57 * 2**20),
        cost_estimate=pl.CostEstimate(
            flops=2 * rows * width * nz * (qcols + kvcols),
            bytes_accessed=2 * rows * width, transcendentals=0),
        name="gather_project_attend",
    )(hidden, q_weight, kv_weight, norm_gain, q_bias, kv_bias, segments)


def positions_of(segments):
    row_ids = jnp.arange(segments.shape[0], dtype=jnp.int32)
    before = jnp.concatenate([jnp.full((1,), -3, jnp.int32), segments[:-1]])
    starts = jnp.where(segments != before, row_ids, 0)
    return row_ids - lax.cummax(starts, axis=0)


def rotate(source, positions):
    half_dim = HEAD_DIM // 2
    frequency = jnp.exp(
        jnp.arange(half_dim, dtype=jnp.float32)
        * (-2.0 / HEAD_DIM)
        * jnp.log(jnp.float32(1000000.0))
    )
    angles = positions.astype(jnp.float32)[:, None] * frequency[None, :]
    cosine = jnp.cos(angles)[:, None, :]
    sine_part = jnp.sin(angles)[:, None, :]
    lower_half = source[..., :half_dim]
    second = source[..., half_dim:]
    return jnp.concatenate(
        [lower_half * cosine - second * sine_part, second * cosine + lower_half * sine_part],
        axis=-1,
    )


def normalize(hidden, norm_gain):
    as_float = hidden.astype(jnp.float32)
    mean_square = jnp.mean(as_float * as_float, axis=-1, keepdims=True)
    return (as_float * lax.rsqrt(mean_square + 1e-06) * norm_gain.astype(jnp.float32)).astype(
        jnp.bfloat16
    )


def windows(source, fill_value):
    block_count = source.shape[0] // BLOCK
    shaped = source.reshape((block_count, BLOCK) + source.shape[1:])
    padded = jnp.concatenate(
        [jnp.full((2,) + shaped.shape[1:], fill_value, source.dtype), shaped], axis=0
    )
    return jnp.concatenate(
        [padded[0:block_count], padded[1 : block_count + 1], padded[2 : block_count + 2]], axis=1
    )


def attend(queries, key_rows, values, segments):
    row_count = queries.shape[0]
    block_count = row_count // BLOCK
    group_size = HEADS // KV_HEADS
    row_ids = jnp.arange(row_count, dtype=jnp.int32)
    key_win = windows(key_rows, 0)
    value_win = windows(values, 0)
    seg_win = windows(segments, -2)
    row_win = windows(row_ids, -1)
    q_blocks = queries.reshape(block_count, BLOCK, KV_HEADS, group_size, HEAD_DIM)
    scores = jnp.einsum(
        "bqkgd,bskd->bkgqs", q_blocks, key_win, preferred_element_type=jnp.float32
    ) * HEAD_DIM ** (-0.5)
    q_seg = segments.reshape(block_count, BLOCK)
    q_row = row_ids.reshape(block_count, BLOCK)
    allowed = (
        (seg_win[:, None, :] == q_seg[:, :, None])
        & (row_win[:, None, :] <= q_row[:, :, None])
        & (q_seg[:, :, None] >= 0)
    )
    scores = jnp.where(allowed[:, None, None], scores, -1e30)
    row_max = jnp.max(scores, axis=-1, keepdims=True)
    exponents = jnp.exp(scores - row_max)
    probabilities = (exponents / jnp.sum(exponents, axis=-1, keepdims=True)).astype(jnp.bfloat16)
    context = jnp.einsum(
        "bkgqs,bskd->bqkgd", probabilities, value_win, preferred_element_type=jnp.float32
    )
    context = jnp.where((q_seg >= 0)[:, :, None, None, None], context, 0.0)
    return context.reshape(row_count, HEADS * HEAD_DIM).astype(jnp.bfloat16)


def project(row_input, positions, q_weight, kv_weight, q_bias, kv_bias):
    row_count = row_input.shape[0]
    q_rows_full, kv_rows_full = (
        lax.all_gather(q_weight, "fsdp", axis=1, tiled=True),
        lax.all_gather(kv_weight, "fsdp", axis=1, tiled=True),
    )

    def add_rows(piece_rows):
        return jnp.dot(row_input, piece_rows, preferred_element_type=jnp.float32)

    q_lin = add_rows(lax.all_gather(q_rows_full, "dp", axis=0, tiled=True))
    kv_lin = add_rows(lax.all_gather(kv_rows_full, "dp", axis=0, tiled=True))
    q_lin = q_lin + q_bias.astype(jnp.float32)
    kv_lin = kv_lin + kv_bias.astype(jnp.float32)
    split_at = KV_HEADS * HEAD_DIM
    queries = rotate(q_lin.reshape(row_count, HEADS, HEAD_DIM), positions).astype(jnp.bfloat16)
    key_rows = rotate(
        kv_lin[:, :split_at].reshape(row_count, KV_HEADS, HEAD_DIM), positions
    ).astype(jnp.bfloat16)
    values = kv_lin[:, split_at:].reshape(row_count, KV_HEADS, HEAD_DIM).astype(jnp.bfloat16)
    return (queries, key_rows, values)


def local(ndp, nz, hidden, norm_gain, q_weight, kv_weight, q_bias, kv_bias, segments):
    planes_fit = ndp == 2 * 2 * 2
    heads_fit = (
        nz == KV_HEADS
        and q_weight.shape[1] == HEADS // KV_HEADS * HEAD_DIM
        and kv_weight.shape[1] == 2 * HEAD_DIM
    )
    if planes_fit and heads_fit:
        return gather_project(
            ndp, nz, hidden, norm_gain, q_weight, kv_weight, q_bias, kv_bias, segments)
    normed = normalize(hidden, norm_gain)
    positions = positions_of(segments)
    queries, key_rows, values = project(normed, positions, q_weight, kv_weight, q_bias, kv_bias)
    return attend(queries, key_rows, values, segments)


def solution(mesh):
    in_specs = (
        P(("dp", "fsdp"), None),
        P(),
        P("dp", "fsdp"),
        P("dp", "fsdp"),
        P(),
        P(),
        P(("dp", "fsdp")),
    )
    out_specs = P(("dp", "fsdp"), None)
    return jax.shard_map(
        functools.partial(local, mesh.shape["dp"], mesh.shape["fsdp"]), mesh=mesh, in_specs=in_specs, out_specs=out_specs, check_vma=False)
```
